32 devices in a mesh: region: 2 (over y), user: 4 (over x, core), item: 4 (over z).
Axes of the slice: x: 2, y: 2, z: 4, core: 2. Of those that a mesh axis runs over, the one named last changes fastest.
Arguments:
- user_emb: bfloat16 [65536, 128], P(('region', 'user')), parts along dimension 0, may hold values from -1.05 to 1.05
- item_emb: bfloat16 [65536, 128], P(('region', 'item')), parts along dimension 0, may hold values from -1.05 to 1.05
- user_count: int32 [65536], P(('region', 'user')), parts along dimension 0, may hold values from 1 to 60, as said below
- item_count: int32 [65536], P(('region', 'item')), parts along dimension 0, may hold values from 1 to 60, as said below
- tiles: int32 [8, 4, 5, 2], P(('region', 'user'), 'item'), parts along dimension 0, may hold values from 0 to 15, as said below
- tile_count: int32 [8, 4], P(('region', 'user'), 'item'), parts along dimension 0, may hold values from 4 to 5, as said below
Outputs:
- user_potential: float32 [65536], P(('region', 'user')), parts along dimension 0
- item_potential: float32 [65536], P(('region', 'item')), parts along dimension 0
The draws below stay inside these ranges and needn't reach their ends.
There are 2 independent parts, one for each index of `region`. The reference program is written for one: setup_inputs(seed, part) draws one part's arguments, and reference() takes and returns one part's arrays. A program takes and returns all parts, laid end to end along the dimension named above; each array names one. Nothing has to cross between parts.
Inputs may be any that keep to these rules, and one draw needn't show every extreme that they name: `tiles`: on the device in user row p and item column q, slot j names a user cluster of that device's user shard and an item cluster of its item shard by local numbers; no pair stands twice on a device. For j < 4 the slot pairs user cluster (q * 4 + j) mod 16 with item cluster (p * 4 + j) mod 16. `tile_count`: the slots in use are the leading ones; the first device uses all 5. `user_count`: positive counts. `item_count`: positive counts.
All inputs are finite; a program needn't handle non-finite values.
Results may differ from the reference program's by a relative error of at most 0.0003.
Values sent between devices are 32-bit elements; how exact they have to be, the bound alone decides.
No kernel may reach another device: no remote copies, remote signals or barrier semaphores. Data moves between devices by JAX's collectives and lax.ppermute only.
A program may use at most 64 MiB of HBM per device.

```python
import jax
import jax.numpy as jnp
from jax import lax

EMBED = 128
CLUSTER = 512
GROUPS_DEV = 16
ITERS = 3
SLOTS = 5
FORCED = 4
USERS = 32768
ITEMS = 32768
N_USER = 4
N_ITEM = 4


def drawn_rows():
    place = jnp.arange(N_ITEM, dtype=jnp.int32)
    return place * GROUPS_DEV * CLUSTER + place * FORCED % GROUPS_DEV * CLUSTER


def item_table(key):
    normal_part = jnp.clip(jax.random.normal(jax.random.fold_in(key, 1), (ITEMS, EMBED), jnp.float32), -3.5, 3.5)
    raw_table = normal_part
    chosen = drawn_rows()
    first_rows = raw_table[chosen]
    second_rows = raw_table[chosen + 1]
    raw_table = raw_table.at[chosen].set(first_rows).at[chosen + 1].set(second_rows)
    return raw_table * EMBED ** (-0.25)


def draw_item_emb(key, part):
    table = item_table(key)
    return table.astype(jnp.bfloat16)


def draw_user_emb(key, part):
    key = jax.random.fold_in(key, 7)
    normal_part = jnp.clip(jax.random.normal(jax.random.fold_in(key, 1), (USERS, EMBED), jnp.float32), -3.5, 3.5)
    users = normal_part * EMBED ** (-0.25)
    chosen = drawn_rows()
    users = users.at[chosen].set(users[chosen])
    return users.astype(jnp.bfloat16)


def draw_user_count(key, part):
    key = jax.random.fold_in(key, 21)
    ramp = 10 + 20 * jnp.arange(USERS, dtype=jnp.int32) // USERS
    return jax.random.randint(key, (USERS,), 1, 2 * ramp + 1, dtype=jnp.int32)


def draw_item_count(key, part):
    key = jax.random.fold_in(key, 22)
    ramp = 10 + 20 * jnp.arange(ITEMS, dtype=jnp.int32) // ITEMS
    return jax.random.randint(key, (ITEMS,), 1, 2 * ramp + 1, dtype=jnp.int32)


def draw_tiles(key, part):
    key = jax.random.fold_in(key, 5)
    grid_size = GROUPS_DEV * GROUPS_DEV
    rows_p = jnp.arange(N_USER, dtype=jnp.int32)[:, None, None]
    cols_q = jnp.arange(N_ITEM, dtype=jnp.int32)[None, :, None]
    lanes = jnp.arange(FORCED, dtype=jnp.int32)[None, None, :]
    fixed_user = jnp.broadcast_to((cols_q * FORCED + lanes) % GROUPS_DEV, (N_USER, N_ITEM, FORCED))
    fixed_item = jnp.broadcast_to((rows_p * FORCED + lanes) % GROUPS_DEV, (N_USER, N_ITEM, FORCED))
    fixed_flat = fixed_user * GROUPS_DEV + fixed_item
    noise = jax.random.randint(key, (N_USER, N_ITEM, grid_size), 0, 1 << 20, dtype=jnp.int32)
    flat_ids = jnp.arange(grid_size, dtype=jnp.int32)
    taken = jnp.any(flat_ids[None, None, :, None] == fixed_flat[:, :, None, :], axis=-1)
    ranking = jnp.where(taken, -1, noise * grid_size + flat_ids[None, None, :])
    _, picked = lax.top_k(ranking, SLOTS - FORCED)
    chosen = jnp.concatenate([fixed_flat, picked.astype(jnp.int32)], axis=-1)
    return jnp.stack([chosen // GROUPS_DEV, chosen % GROUPS_DEV], axis=-1).astype(jnp.int32)


def draw_tile_count(key, part):
    key = jax.random.fold_in(key, 23)
    drawn = jax.random.randint(key, (N_USER, N_ITEM), FORCED, SLOTS + 1, dtype=jnp.int32)
    first = (jnp.arange(N_USER)[:, None] == 0) & (jnp.arange(N_ITEM)[None, :] == 0)
    return jnp.where(first, SLOTS, drawn).astype(jnp.int32)


def setup_inputs(seed: int = 0, part: int = 0) -> dict:
    keys = jax.random.split(jax.random.key(seed), 7)
    part_splits = jax.random.split(jax.random.fold_in(keys[6], part), 7)
    return {
        "user_emb": draw_user_emb(jax.random.fold_in(jax.random.fold_in(keys[6], part), 71), part),
        "item_emb": draw_item_emb(jax.random.fold_in(jax.random.fold_in(keys[6], part), 71), part),
        "user_count": draw_user_count(jax.random.fold_in(jax.random.fold_in(keys[6], part), 71), part),
        "item_count": draw_item_count(jax.random.fold_in(jax.random.fold_in(keys[6], part), 71), part),
        "tiles": draw_tiles(jax.random.fold_in(jax.random.fold_in(keys[6], part), 71), part),
        "tile_count": draw_tile_count(jax.random.fold_in(jax.random.fold_in(keys[6], part), 71), part),
    }


entropy = 0.25
lowest = -1e30


def half_step(row_table, col_table, col_values, row_starts, col_starts, usable, rows_total):
    def advance(state, entry):
        top_rows, mass_rows = state
        row_start, col_start, active = entry
        row_block = lax.dynamic_slice_in_dim(row_table, row_start, CLUSTER, 0).astype(jnp.float32)
        col_block = lax.dynamic_slice_in_dim(col_table, col_start, CLUSTER, 0).astype(jnp.float32)
        shifts = lax.dynamic_slice_in_dim(col_values, col_start, CLUSTER, 0)
        products = jnp.dot(row_block, col_block.T, precision=lax.Precision.HIGHEST)
        scores = (products + shifts[None, :]) / entropy
        tile_top = jnp.max(scores, axis=1)
        tile_mass = jnp.sum(jnp.exp(scores - tile_top[:, None]), axis=1)
        old_top = lax.dynamic_slice_in_dim(top_rows, row_start, CLUSTER, 0)
        old_mass = lax.dynamic_slice_in_dim(mass_rows, row_start, CLUSTER, 0)
        new_top = jnp.maximum(old_top, tile_top)
        new_mass = old_mass * jnp.exp(old_top - new_top) + tile_mass * jnp.exp(tile_top - new_top)
        new_top = jnp.where(active, new_top, old_top)
        new_mass = jnp.where(active, new_mass, old_mass)
        top_rows = lax.dynamic_update_slice_in_dim(top_rows, new_top, row_start, 0)
        mass_rows = lax.dynamic_update_slice_in_dim(mass_rows, new_mass, row_start, 0)
        return (top_rows, mass_rows), None

    start = (jnp.full((rows_total,), lowest, jnp.float32), jnp.zeros((rows_total,), jnp.float32))
    (top_rows, mass_rows), _ = lax.scan(advance, start, (row_starts, col_starts, usable))
    return top_rows + jnp.log(mass_rows)


def reference(user_emb, item_emb, user_count, item_count, tiles, tile_count):
    rows_dev = GROUPS_DEV * CLUSTER
    grid_user = jnp.arange(N_USER, dtype=jnp.int32)[:, None, None]
    grid_item = jnp.arange(N_ITEM, dtype=jnp.int32)[None, :, None]
    slot_ids = jnp.arange(SLOTS, dtype=jnp.int32)[None, None, :]
    user_starts = (grid_user * rows_dev + tiles[:, :, :, 0] * CLUSTER).reshape(-1).astype(jnp.int32)
    item_starts = (grid_item * rows_dev + tiles[:, :, :, 1] * CLUSTER).reshape(-1).astype(jnp.int32)
    usable = (slot_ids < tile_count[:, :, None]).reshape(-1)
    user_counts = user_count.astype(jnp.float32)
    item_counts = item_count.astype(jnp.float32)
    log_users = jnp.log(user_counts / jnp.sum(user_counts))
    log_items = jnp.log(item_counts / jnp.sum(item_counts))
    item_values = jnp.zeros((ITEMS,), jnp.float32)
    user_values = jnp.zeros((USERS,), jnp.float32)
    for iteration in range(ITERS):
        user_values = entropy * (log_users - half_step(user_emb, item_emb, item_values, user_starts, item_starts, usable, USERS))
        item_values = entropy * (log_items - half_step(item_emb, user_emb, user_values, item_starts, user_starts, usable, ITEMS))
    return user_values, item_values
```

```python
import math

import jax
import jax.numpy as jnp
from jax import lax
from jax.experimental import pallas as pl
from jax.experimental.pallas import tpu as pltpu
from jax.sharding import PartitionSpec as P

CLUSTER = 512
LANES = 128
BLOCKS = CLUSTER // LANES
ROWS = 8
ITERS = 3
entropy = 0.25
lowest = -1e30
INTO = math.log2(math.e) / entropy
BACK = entropy * math.log(2.0)

HERE = pl.BlockSpec(memory_space=pltpu.VMEM)
SCALARS = pl.BlockSpec(memory_space=pltpu.SMEM)
FAR = pl.BlockSpec(memory_space=pltpu.HBM)
PACK = (ROWS, CLUSTER)


def near(shape, dtype=jnp.float32):
    return pltpu.VMEM(shape, dtype)


def keep(array):
    return pltpu.with_memory_space_constraint(array, pltpu.VMEM)


def note_at(slots, number):
    row = slots + number // BLOCKS
    lane = number % BLOCKS * LANES
    return slice(row, row + 1), slice(lane, lane + LANES)


def wide(block):
    return jnp.concatenate([block] * BLOCKS, axis=1)


def total_of(counts):
    total = jnp.sum(jnp.sum(counts.astype(jnp.float32), axis=0, keepdims=True), axis=1, keepdims=True)
    return jnp.broadcast_to(total, (1, LANES))


def write_notes(pack, tiles, which, counts):
    slots = tiles.shape[2]
    pack[slots:, :] = jnp.zeros((ROWS - slots, CLUSTER), jnp.float32)
    for slot in range(slots):
        number = jnp.full((1, LANES), tiles[0, 0, slot, which], jnp.int32)
        pack[note_at(slots, slot)] = number.astype(jnp.float32)
    pack[note_at(slots, slots)] = total_of(counts)


def first_kernel(tiles, filled, user_emb, item_emb, item_count, pack, users, items, scores, sems):
    slots = tiles.shape[2]
    copies = []
    for slot in range(slots):
        pair = []
        for which, (table, into) in enumerate(((user_emb, users), (item_emb, items))):
            start = pl.multiple_of(tiles[0, 0, slot, which] * CLUSTER, CLUSTER)
            copy = pltpu.make_async_copy(
                table.at[pl.ds(start, CLUSTER)], into.at[slot], sems.at[slot, which]
            )
            copy.start()
            pair.append(copy)
        copies.append(pair)
    write_notes(pack, tiles, 0, item_count[...])
    for slot in range(slots):
        for copy in copies[slot]:
            copy.wait()
        user_block = users[slot]
        top = jnp.full((8, CLUSTER), lowest, jnp.float32)
        for block in range(BLOCKS):
            rows = slice(block * LANES, (block + 1) * LANES)
            part = lax.dot_general(
                items[slot, rows, :], user_block, (((1,), (1,)), ((), ())),
                preferred_element_type=jnp.float32,
            ) * INTO
            scores[rows, :] = part
            top = jnp.maximum(top, jnp.max(part.reshape(LANES // 8, 8, CLUSTER), axis=0))
        top = jnp.max(top, axis=0, keepdims=True)
        mass = jnp.zeros((8, CLUSTER), jnp.float32)
        for block in range(BLOCKS):
            rows = slice(block * LANES, (block + 1) * LANES)
            terms = jnp.exp2(scores[rows, :] - top)
            mass += jnp.sum(terms.reshape(LANES // 8, 8, CLUSTER), axis=0)
        log_mass = top + jnp.log2(jnp.sum(mass, axis=0, keepdims=True))
        pack[slot : slot + 1, :] = jnp.where(filled[0, 0] > slot, log_mass, lowest)


def setup_kernel(
    tiles, filled, users, items, user_count, item_count,
    table, user_here, item_here, user_ids, item_ids, notes, active,
):
    slots = tiles.shape[2]
    for slot in range(slots):
        item_block = items[slot]
        for block in range(BLOCKS):
            rows = slice(block * LANES, (block + 1) * LANES)
            table[slot, rows, :] = lax.dot_general(
                users[slot, rows, :], item_block, (((1,), (1,)), ((), ())),
                preferred_element_type=jnp.float32,
            ) * INTO
    place = lax.broadcasted_iota(jnp.int32, (ROWS, LANES), 0)
    on = jnp.where(place < filled[0, 0], 1.0, 0.0)
    active[...] = wide(on)
    for which, (counts, here, ids) in enumerate(
        ((user_count, user_here, user_ids), (item_count, item_here, item_ids))
    ):
        numbers = jnp.full((ROWS, LANES), -1, jnp.int32)
        here[...] = jnp.ones(PACK, jnp.float32)
        for slot in range(slots):
            group = tiles[0, 0, slot, which]
            numbers = jnp.where(place == slot, group, numbers)
            for block in range(BLOCKS):
                here[slot : slot + 1, block * LANES : (block + 1) * LANES] = counts[
                    pl.ds(group * BLOCKS + block, 1), :
                ].astype(jnp.float32)
        ids[...] = numbers.astype(jnp.float32)
    notes[...] = jnp.zeros(PACK, jnp.float32)
    write_notes(notes, tiles, 1, user_count[...])


def matches(packs, ids, slots):
    return [
        [ids == pack[note_at(slots, slot)] for slot in range(slots)] for pack in packs
    ]


def log_merge(packs, chosen, slots, lanes, rows):
    width = lanes.stop - lanes.start
    spread = wide if width == CLUSTER else (lambda mask: mask)
    top = jnp.full((rows, width), lowest, jnp.float32)
    for pack, masks in zip(packs, chosen):
        for slot in range(slots):
            part = jnp.where(spread(masks[slot]), pack[slot : slot + 1, lanes], lowest)
            top = jnp.maximum(top, part)
    mass = jnp.zeros((rows, width), jnp.float32)
    for pack, masks in zip(packs, chosen):
        for slot in range(slots):
            part = jnp.exp2(pack[slot : slot + 1, lanes] - top)
            mass += jnp.where(spread(masks[slot]), part, 0.0)
    return top + jnp.log2(jnp.where(mass > 0.0, mass, 1.0))


def sum_merge(packs, chosen, slots, lanes, rows):
    width = lanes.stop - lanes.start
    spread = wide if width == CLUSTER else (lambda mask: mask)
    total = jnp.zeros((rows, width), jnp.float32)
    for pack, masks in zip(packs, chosen):
        for slot in range(slots):
            total += jnp.where(spread(masks[slot]), pack[slot : slot + 1, lanes], 0.0)
    return total


def total_in(packs, slots):
    total = packs[0][note_at(slots, slots)]
    for pack in packs[1:]:
        total = total + pack[note_at(slots, slots)]
    return total


def store_masks(masks, chosen):
    for index, mask in enumerate(mask for group in chosen for mask in group):
        masks[index] = jnp.where(mask, 1.0, 0.0)


def load_masks(masks, devices, slots):
    return [
        [masks[device * slots + slot] > 0.0 for slot in range(slots)] for device in range(devices)
    ]


def down_rows(vector, slot, block):
    row = vector[slot : slot + 1, block * LANES : (block + 1) * LANES]
    return jnp.broadcast_to(row, (LANES, LANES)).T


EVERY = slice(0, CLUSTER)


def second_kernel(devices, *refs):
    packs = refs[:devices]
    table, ids, counts, notes, active, pack, terms, tops, masks, totals, potential = refs[devices:]
    slots = table.shape[0]
    chosen = matches(packs, ids[...], slots)
    store_masks(masks, chosen)
    totals[...] = jnp.broadcast_to(total_in(packs, slots), totals.shape)
    potential[...] = jnp.log2(counts[...]) - log_merge(packs, chosen, slots, EVERY, ROWS)
    pack[...] = notes[...]
    tops[...] = jnp.full(PACK, lowest, jnp.float32)
    for slot in range(slots):
        top = jnp.full((8, CLUSTER), lowest, jnp.float32)
        for block in range(BLOCKS):
            rows = slice(block * LANES, (block + 1) * LANES)
            part = table[slot, rows, :] + wide(down_rows(potential, slot, block))
            terms[slot, rows, :] = part
            top = jnp.maximum(top, jnp.max(part.reshape(LANES // 8, 8, CLUSTER), axis=0))
        top = jnp.max(top, axis=0, keepdims=True)
        mass = jnp.zeros((8, CLUSTER), jnp.float32)
        for block in range(BLOCKS):
            rows = slice(block * LANES, (block + 1) * LANES)
            part = jnp.exp2(terms[slot, rows, :] - top)
            terms[slot, rows, :] = part
            mass += jnp.sum(part.reshape(LANES // 8, 8, CLUSTER), axis=0)
        log_mass = top + jnp.log2(jnp.sum(mass, axis=0, keepdims=True))
        on = active[slot : slot + 1, :] > 0.0
        pack[slot : slot + 1, :] = jnp.where(on, log_mass, lowest)
        tops[slot : slot + 1, :] = jnp.where(on, top, lowest)


def row_sums(terms, factor, pack):
    slots = terms.shape[0]
    pack[...] = jnp.zeros(PACK, jnp.float32)
    for slot in range(slots):
        for block in range(BLOCKS):
            rows = slice(block * LANES, (block + 1) * LANES)
            part = terms[slot, rows, 0:LANES] * factor[slot : slot + 1, 0:LANES]
            for other in range(1, BLOCKS):
                lanes = slice(other * LANES, (other + 1) * LANES)
                part += terms[slot, rows, lanes] * factor[slot : slot + 1, lanes]
            pack[slot : slot + 1, rows] = jnp.sum(part.T, axis=0, keepdims=True)


def column_sums(terms, factor, scale, pack):
    slots = terms.shape[0]
    pack[...] = jnp.zeros(PACK, jnp.float32)
    for slot in range(slots):
        mass = jnp.zeros((8, CLUSTER), jnp.float32)
        for block in range(BLOCKS):
            rows = slice(block * LANES, (block + 1) * LANES)
            part = terms[slot, rows, :] * wide(down_rows(factor, slot, block))
            mass += jnp.sum(part.reshape(LANES // 8, 8, CLUSTER), axis=0)
        pack[slot : slot + 1, :] = jnp.sum(mass, axis=0, keepdims=True) * scale[slot : slot + 1, :]


def third_kernel(devices, *refs):
    packs = refs[:devices]
    terms, tops, ids, counts, item_total, pack, factor, masks, totals = refs[devices:]
    slots = terms.shape[0]
    chosen = matches(packs, ids[...], slots)
    store_masks(masks, chosen)
    totals[...] = jnp.broadcast_to(total_in(packs, slots), totals.shape)
    log_share = jnp.log2(counts[...] / wide(item_total[...]))
    merged = log_merge(packs, chosen, slots, EVERY, ROWS)
    factor[...] = jnp.exp2(tops[...] + (log_share - merged))
    row_sums(terms, factor, pack)


def user_kernel(devices, *refs):
    packs = refs[:devices]
    terms, masks, counts, totals, scale, pack, factor = refs[devices:]
    slots = terms.shape[0]
    sums = sum_merge(packs, load_masks(masks, devices, slots), slots, EVERY, ROWS)
    factor[...] = counts[...] / (wide(totals[...]) * jnp.where(sums > 0.0, sums, 1.0))
    column_sums(terms, factor, scale, pack)


def item_kernel(devices, *refs):
    packs = refs[:devices]
    terms, masks, counts, totals, old, pack, factor = refs[devices:]
    slots = terms.shape[0]
    sums = sum_merge(packs, load_masks(masks, devices, slots), slots, EVERY, ROWS)
    share = counts[...] / (wide(totals[...]) * jnp.where(sums > 0.0, sums, 1.0))
    factor[...] = old[...] * share
    row_sums(terms, factor, pack)


def in_order(axis, devices, packs, ordered):
    me = lax.axis_index(axis)
    for step in range(devices):
        ordered[source(me, step, devices)] = packs[step][...]
    return [ordered.at[device] for device in range(devices)]


def cluster_matches(packs, slots, groups):
    numbers = lax.broadcasted_iota(jnp.int32, (groups, LANES), 0).astype(jnp.float32)
    return matches(packs, numbers, slots)


def user_out_kernel(axis, devices, slots, *refs):
    counts, totals, out, first_packs, last_packs = refs[2 * devices :]
    first = in_order(axis, devices, refs[:devices], first_packs)
    last = in_order(axis, devices, refs[devices : 2 * devices], last_packs)
    groups = counts.shape[0] // BLOCKS
    chosen = cluster_matches(first, slots, groups)
    for block in range(BLOCKS):
        lanes = slice(block * LANES, (block + 1) * LANES)
        here = pl.ds(block, groups, stride=BLOCKS)
        share = jnp.log2(counts[here, :].astype(jnp.float32) / totals[0:1, :])
        merged = log_merge(first, chosen, slots, lanes, groups)
        sums = sum_merge(last, chosen, slots, lanes, groups)
        out[here, :] = BACK * (2.0 * share - merged - jnp.log2(sums))


def item_base_kernel(axis, devices, slots, middles, *refs):
    given = (1 + middles) * devices
    counts, item_total, user_total, out, numbers, all_packs = refs[given:]
    packs = [
        in_order(axis, devices, refs[step * devices : (step + 1) * devices], all_packs.at[step])
        for step in range(1 + middles)
    ]
    groups = counts.shape[0] // BLOCKS
    chosen = cluster_matches(packs[0], slots, groups)
    for index, mask in enumerate(mask for group in chosen for mask in group):
        numbers[index] = jnp.where(mask, 1.0, 0.0)
    for block in range(BLOCKS):
        lanes = slice(block * LANES, (block + 1) * LANES)
        here = pl.ds(block, groups, stride=BLOCKS)
        share = jnp.log2(counts[here, :].astype(jnp.float32) / item_total[0:1, :])
        base = (2 + middles) * share + jnp.log2(user_total[0:1, :])
        base = base - log_merge(packs[0], chosen, slots, lanes, groups)
        for step in range(middles):
            base = base - jnp.log2(sum_merge(packs[1 + step], chosen, slots, lanes, groups))
        out[here, :] = base


def item_out_kernel(axis, devices, slots, *refs):
    base, numbers, out, packs_here = refs[devices:]
    packs = in_order(axis, devices, refs[:devices], packs_here)
    groups = base.shape[0] // BLOCKS
    chosen = load_masks(numbers, devices, slots)
    for block in range(BLOCKS):
        lanes = slice(block * LANES, (block + 1) * LANES)
        here = pl.ds(block, groups, stride=BLOCKS)
        sums = sum_merge(packs, chosen, slots, lanes, groups)
        out[here, :] = BACK * (base[here, :] - jnp.log2(sums))


def paired(devices):
    return devices & (devices - 1) == 0


def source(me, step, devices):
    if paired(devices):
        return jnp.bitwise_xor(me, step)
    return lax.rem(me + devices - step, devices)


def exchange(pack, axis, devices):
    packs = [pack]
    for step in range(1, devices):
        if paired(devices):
            route = [(device, device ^ step) for device in range(devices)]
        else:
            route = [(device, (device + step) % devices) for device in range(devices)]
        packs.append(keep(lax.ppermute(pack, axis, route)))
    return packs


def call(kernel, outs, operands, specs=None, scratch=(), **params):
    return pl.pallas_call(
        kernel,
        out_shape=outs,
        in_specs=specs or [HERE] * len(operands),
        out_specs=jax.tree.map(lambda _: HERE, outs, is_leaf=lambda leaf: not isinstance(leaf, list)),
        scratch_shapes=list(scratch),
        compiler_params=pltpu.CompilerParams(vmem_limit_bytes=16 << 20),
        **params,
    )(*operands)


def bind(kernel, *fixed):
    return lambda *refs: kernel(*fixed, *refs)


def make_body(n_user, n_item):
    def body(user_emb, item_emb, user_count, item_count, tiles, tile_count):
        slots = tiles.shape[2]
        tall = (slots, CLUSTER, CLUSTER)
        vectors = near(PACK)
        splat = near((ROWS, LANES))
        user_counts = user_count.reshape(-1, LANES)
        item_counts = item_count.reshape(-1, LANES)
        gathered = near((slots, CLUSTER, user_emb.shape[1]), user_emb.dtype)

        pack, users, items = call(
            first_kernel,
            [vectors, gathered, gathered],
            (tiles, tile_count, user_emb, item_emb, item_counts),
            [SCALARS, SCALARS, FAR, FAR, HERE],
            [near((CLUSTER, CLUSTER)), pltpu.SemaphoreType.DMA((slots, 2))],
        )
        first_packs = exchange(pack, "item", n_item)
        table, user_here, item_here, user_ids, item_ids, notes, active = call(
            setup_kernel,
            [near(tall), vectors, vectors, splat, splat, vectors, vectors],
            (tiles, tile_count, keep(users), keep(items), user_counts, item_counts),
            [SCALARS, SCALARS, HERE, HERE, HERE, HERE],
        )
        pack, terms, tops, user_masks, item_total = call(
            bind(second_kernel, n_item),
            [vectors, near(tall), vectors, near((n_item * slots, ROWS, LANES)), splat],
            (*first_packs, keep(table), user_ids, user_here, notes, active),
            scratch=[near(PACK)],
        )
        terms = keep(terms)
        second_packs = exchange(pack, "user", n_user)
        pack, factor, item_masks, user_total = call(
            bind(third_kernel, n_user),
            [vectors, vectors, near((n_user * slots, ROWS, LANES)), splat],
            (*second_packs, terms, tops, item_ids, item_here, item_total),
        )
        item_packs = [second_packs]
        for iteration in range(1, ITERS):
            user_packs = exchange(pack, "item", n_item)
            (pack,) = call(
                bind(user_kernel, n_item),
                [vectors],
                (*user_packs, terms, user_masks, user_here, user_total, factor),
                scratch=[near(PACK)],
            )
            item_packs.append(exchange(pack, "user", n_user))
            if iteration < ITERS - 1:
                pack, factor = call(
                    bind(item_kernel, n_user),
                    [vectors, vectors],
                    (*item_packs[-1], terms, item_masks, item_here, item_total, factor),
                )
        user_values = call(
            bind(user_out_kernel, "item", n_item, slots),
            jax.ShapeDtypeStruct(user_counts.shape, jnp.float32),
            (*first_packs, *user_packs, user_counts, user_total),
            scratch=[near((n_item, *PACK)), near((n_item, *PACK))],
        )
        middles = ITERS - 2
        groups = item_counts.shape[0] // BLOCKS
        base, numbers = call(
            bind(item_base_kernel, "user", n_user, slots, middles),
            [near(item_counts.shape), near((n_user * slots, groups, LANES))],
            (*(pack for packs in item_packs[:-1] for pack in packs), item_counts, item_total, user_total),
            scratch=[near((1 + middles, n_user, *PACK))],
        )
        item_values = call(
            bind(item_out_kernel, "user", n_user, slots),
            jax.ShapeDtypeStruct(item_counts.shape, jnp.float32),
            (*item_packs[-1], base, numbers),
            scratch=[near((n_user, *PACK))],
        )
        return user_values.reshape(-1), item_values.reshape(-1)

    return body


def solution(mesh):
    in_specs = (
        P(("region", "user"), None),
        P(("region", "item"), None),
        P(("region", "user")),
        P(("region", "item")),
        P(("region", "user"), "item", None, None),
        P(("region", "user"), "item"),
    )
    out_specs = (P(("region", "user")), P(("region", "item")))
    return jax.shard_map(
        make_body(mesh.shape["user"], mesh.shape["item"]),
        mesh=mesh,
        in_specs=in_specs,
        out_specs=out_specs,
        check_vma=False,
    )
```

```python
import math

import jax
import jax.numpy as jnp
from jax import lax
from jax.experimental import pallas as pl
from jax.experimental.pallas import tpu as pltpu
from jax.sharding import PartitionSpec as P

CLUSTER = 512
LANES = 128
BLOCKS = CLUSTER // LANES
ROWS = 8
ITERS = 3
entropy = 0.25
lowest = -1e30
INTO = math.log2(math.e) / entropy
BACK = entropy * math.log(2.0)

HERE = pl.BlockSpec(memory_space=pltpu.VMEM)
SCALARS = pl.BlockSpec(memory_space=pltpu.SMEM)
FAR = pl.BlockSpec(memory_space=pltpu.HBM)
PACK = (ROWS, CLUSTER)


def near(shape, dtype=jnp.float32):
    return pltpu.VMEM(shape, dtype)


def keep(array):
    return pltpu.with_memory_space_constraint(array, pltpu.VMEM)


def away(array):
    return pltpu.with_memory_space_constraint(array, pltpu.HBM)


def note_at(slots, number):
    row = slots + number // BLOCKS
    lane = number % BLOCKS * LANES
    return slice(row, row + 1), slice(lane, lane + LANES)


def wide(block):
    return jnp.concatenate([block] * BLOCKS, axis=1)


def total_of(counts):
    total = jnp.sum(jnp.sum(counts.astype(jnp.float32), axis=0, keepdims=True), axis=1, keepdims=True)
    return jnp.broadcast_to(total, (1, LANES))


def write_notes(pack, tiles, which, counts):
    slots = tiles.shape[1]
    pack[slots:, :] = jnp.zeros((ROWS - slots, CLUSTER), jnp.float32)
    for slot in range(slots):
        number = jnp.full((1, LANES), tiles[which, slot], jnp.int32)
        pack[note_at(slots, slot)] = number.astype(jnp.float32)
    pack[note_at(slots, slots)] = total_of(counts)


def first_kernel(
    devices, far_tiles, filled, user_emb, item_emb, far_count, pack, users, items,
    tiles, item_count, scores, small_sems, sems,
):
    slots = tiles.shape[1]
    groups = user_emb.shape[0] // CLUSTER
    small = [
        pltpu.make_async_copy(source, target, small_sems.at[index])
        for index, (source, target) in enumerate(
            ((far_tiles, tiles), (far_count, item_count))
        )
    ]
    for copy in small:
        copy.start()

    def fetch(slot, groups_here):
        pair = []
        for which, (table, into) in enumerate(((user_emb, users), (item_emb, items))):
            start = pl.multiple_of(groups_here[which] * CLUSTER, CLUSTER)
            copy = pltpu.make_async_copy(
                table.at[pl.ds(start, CLUSTER)], into.at[slot], sems.at[slot, which]
            )
            copy.start()
            pair.append(copy)
        return pair

    n_user, n_item = devices
    fixed = min(groups // n_user, groups // n_item, slots)
    row, column = lax.axis_index("user"), lax.axis_index("item")
    copies = [
        fetch(slot, [lax.rem(place * fixed + slot, groups) for place in (column, row)])
        for slot in range(fixed)
    ]
    for copy in small:
        copy.wait()
    for slot in range(fixed, slots):
        copies.append(fetch(slot, [tiles[which, slot] for which in range(2)]))
    write_notes(pack, tiles, 0, item_count[...])
    for slot in range(slots):
        for copy in copies[slot]:
            copy.wait()
        user_block = users[slot]
        top = jnp.full((8, CLUSTER), lowest, jnp.float32)
        for block in range(BLOCKS):
            rows = slice(block * LANES, (block + 1) * LANES)
            part = lax.dot_general(
                items[slot, rows, :], user_block, (((1,), (1,)), ((), ())),
                preferred_element_type=jnp.float32,
            ) * INTO
            scores[rows, :] = part
            top = jnp.maximum(top, jnp.max(part.reshape(LANES // 8, 8, CLUSTER), axis=0))
        top = jnp.max(top, axis=0, keepdims=True)
        mass = jnp.zeros((8, CLUSTER), jnp.float32)
        for block in range(BLOCKS):
            rows = slice(block * LANES, (block + 1) * LANES)
            terms = jnp.exp2(scores[rows, :] - top)
            mass += jnp.sum(terms.reshape(LANES // 8, 8, CLUSTER), axis=0)
        log_mass = top + jnp.log2(jnp.sum(mass, axis=0, keepdims=True))
        pack[slot : slot + 1, :] = jnp.where(filled[0, 0] > slot, log_mass, lowest)


def setup_kernel(
    far_tiles, filled, users, items, far_users, far_items,
    table, user_here, item_here, user_ids, item_ids, notes, active,
    tiles, user_count, item_count, sems,
):
    slots = tiles.shape[1]
    copies = [
        pltpu.make_async_copy(source, target, sems.at[index])
        for index, (source, target) in enumerate(
            (
                (far_tiles, tiles),
                (far_users, user_count),
                (far_items, item_count),
            )
        )
    ]
    for copy in copies:
        copy.start()
    for slot in range(slots):
        item_block = items[slot]
        for block in range(BLOCKS):
            rows = slice(block * LANES, (block + 1) * LANES)
            table[slot, rows, :] = lax.dot_general(
                users[slot, rows, :], item_block, (((1,), (1,)), ((), ())),
                preferred_element_type=jnp.float32,
            ) * INTO
    for copy in copies:
        copy.wait()
    place = lax.broadcasted_iota(jnp.int32, (ROWS, LANES), 0)
    on = jnp.where(place < filled[0, 0], 1.0, 0.0)
    active[...] = wide(on)
    for which, (counts, here, ids) in enumerate(
        ((user_count, user_here, user_ids), (item_count, item_here, item_ids))
    ):
        numbers = jnp.full((ROWS, LANES), -1, jnp.int32)
        here[...] = jnp.ones(PACK, jnp.float32)
        for slot in range(slots):
            group = tiles[which, slot]
            numbers = jnp.where(place == slot, group, numbers)
            for block in range(BLOCKS):
                here[slot : slot + 1, block * LANES : (block + 1) * LANES] = counts[
                    pl.ds(group * BLOCKS + block, 1), :
                ].astype(jnp.float32)
        ids[...] = numbers.astype(jnp.float32)
    notes[...] = jnp.zeros(PACK, jnp.float32)
    write_notes(notes, tiles, 1, user_count[...])


def matches(packs, ids, slots):
    return [
        [ids == pack[note_at(slots, slot)] for slot in range(slots)] for pack in packs
    ]


def log_merge(packs, chosen, slots, lanes, rows):
    width = lanes.stop - lanes.start
    spread = wide if width == CLUSTER else (lambda mask: mask)
    top = jnp.full((rows, width), lowest, jnp.float32)
    for pack, masks in zip(packs, chosen):
        for slot in range(slots):
            part = jnp.where(spread(masks[slot]), pack[slot : slot + 1, lanes], lowest)
            top = jnp.maximum(top, part)
    mass = jnp.zeros((rows, width), jnp.float32)
    for pack, masks in zip(packs, chosen):
        for slot in range(slots):
            part = jnp.exp2(pack[slot : slot + 1, lanes] - top)
            mass += jnp.where(spread(masks[slot]), part, 0.0)
    return top + jnp.log2(jnp.where(mass > 0.0, mass, 1.0))


def sum_merge(packs, chosen, slots, lanes, rows):
    width = lanes.stop - lanes.start
    spread = wide if width == CLUSTER else (lambda mask: mask)
    total = jnp.zeros((rows, width), jnp.float32)
    for pack, masks in zip(packs, chosen):
        for slot in range(slots):
            total += jnp.where(spread(masks[slot]), pack[slot : slot + 1, lanes], 0.0)
    return total


def total_in(packs, slots):
    total = packs[0][note_at(slots, slots)]
    for pack in packs[1:]:
        total = total + pack[note_at(slots, slots)]
    return total


def store_masks(masks, chosen):
    for index, mask in enumerate(mask for group in chosen for mask in group):
        masks[index] = jnp.where(mask, 1.0, 0.0)


def load_masks(masks, devices, slots):
    return [
        [masks[device * slots + slot] > 0.0 for slot in range(slots)] for device in range(devices)
    ]


def down_rows(vector, slot, block):
    row = vector[slot : slot + 1, block * LANES : (block + 1) * LANES]
    return jnp.broadcast_to(row, (LANES, LANES)).T


EVERY = slice(0, CLUSTER)


def second_kernel(devices, *refs):
    packs = refs[:devices]
    table, ids, counts, notes, active, pack, terms, tops, masks, totals, potential = refs[devices:]
    slots = table.shape[0]
    chosen = matches(packs, ids[...], slots)
    store_masks(masks, chosen)
    totals[...] = jnp.broadcast_to(total_in(packs, slots), totals.shape)
    potential[...] = jnp.log2(counts[...]) - log_merge(packs, chosen, slots, EVERY, ROWS)
    pack[...] = notes[...]
    tops[...] = jnp.full(PACK, lowest, jnp.float32)
    for slot in range(slots):
        top = jnp.full((8, CLUSTER), lowest, jnp.float32)
        for block in range(BLOCKS):
            rows = slice(block * LANES, (block + 1) * LANES)
            part = table[slot, rows, :] + wide(down_rows(potential, slot, block))
            terms[slot, rows, :] = part
            top = jnp.maximum(top, jnp.max(part.reshape(LANES // 8, 8, CLUSTER), axis=0))
        top = jnp.max(top, axis=0, keepdims=True)
        mass = jnp.zeros((8, CLUSTER), jnp.float32)
        for block in range(BLOCKS):
            rows = slice(block * LANES, (block + 1) * LANES)
            part = jnp.exp2(terms[slot, rows, :] - top)
            terms[slot, rows, :] = part
            mass += jnp.sum(part.reshape(LANES // 8, 8, CLUSTER), axis=0)
        log_mass = top + jnp.log2(jnp.sum(mass, axis=0, keepdims=True))
        on = active[slot : slot + 1, :] > 0.0
        pack[slot : slot + 1, :] = jnp.where(on, log_mass, lowest)
        tops[slot : slot + 1, :] = jnp.where(on, top, lowest)


def row_sums(terms, factor, pack):
    slots = terms.shape[0]
    pack[...] = jnp.zeros(PACK, jnp.float32)
    for slot in range(slots):
        for block in range(BLOCKS):
            rows = slice(block * LANES, (block + 1) * LANES)
            part = terms[slot, rows, 0:LANES] * factor[slot : slot + 1, 0:LANES]
            for other in range(1, BLOCKS):
                lanes = slice(other * LANES, (other + 1) * LANES)
                part += terms[slot, rows, lanes] * factor[slot : slot + 1, lanes]
            pack[slot : slot + 1, rows] = jnp.sum(part.T, axis=0, keepdims=True)


def column_sums(terms, factor, scale, pack):
    slots = terms.shape[0]
    pack[...] = jnp.zeros(PACK, jnp.float32)
    for slot in range(slots):
        mass = jnp.zeros((8, CLUSTER), jnp.float32)
        for block in range(BLOCKS):
            rows = slice(block * LANES, (block + 1) * LANES)
            part = terms[slot, rows, :] * wide(down_rows(factor, slot, block))
            mass += jnp.sum(part.reshape(LANES // 8, 8, CLUSTER), axis=0)
        pack[slot : slot + 1, :] = jnp.sum(mass, axis=0, keepdims=True) * scale[slot : slot + 1, :]


def third_kernel(devices, *refs):
    packs = refs[:devices]
    terms, tops, ids, counts, item_total, pack, factor, masks, totals = refs[devices:]
    slots = terms.shape[0]
    chosen = matches(packs, ids[...], slots)
    store_masks(masks, chosen)
    totals[...] = jnp.broadcast_to(total_in(packs, slots), totals.shape)
    log_share = jnp.log2(counts[...] / wide(item_total[...]))
    merged = log_merge(packs, chosen, slots, EVERY, ROWS)
    factor[...] = jnp.exp2(tops[...] + (log_share - merged))
    row_sums(terms, factor, pack)


def user_kernel(devices, *refs):
    packs = refs[:devices]
    terms, masks, counts, totals, scale, pack, factor = refs[devices:]
    slots = terms.shape[0]
    sums = sum_merge(packs, load_masks(masks, devices, slots), slots, EVERY, ROWS)
    factor[...] = counts[...] / (wide(totals[...]) * jnp.where(sums > 0.0, sums, 1.0))
    column_sums(terms, factor, scale, pack)


def item_kernel(devices, *refs):
    packs = refs[:devices]
    terms, masks, counts, totals, old, pack, factor = refs[devices:]
    slots = terms.shape[0]
    sums = sum_merge(packs, load_masks(masks, devices, slots), slots, EVERY, ROWS)
    share = counts[...] / (wide(totals[...]) * jnp.where(sums > 0.0, sums, 1.0))
    factor[...] = old[...] * share
    row_sums(terms, factor, pack)


def in_order(axis, devices, packs, ordered):
    me = lax.axis_index(axis)
    for step in range(devices):
        ordered[partner(me, step, devices)] = packs[step][...]
    return [ordered.at[device] for device in range(devices)]


def cluster_matches(packs, slots, groups):
    numbers = lax.broadcasted_iota(jnp.int32, (groups, LANES), 0).astype(jnp.float32)
    return matches(packs, numbers, slots)


def user_out_kernel(axis, devices, slots, *refs):
    counts, totals, out, first_packs, last_packs = refs[2 * devices :]
    first = in_order(axis, devices, refs[:devices], first_packs)
    last = in_order(axis, devices, refs[devices : 2 * devices], last_packs)
    groups = counts.shape[0] // BLOCKS
    chosen = cluster_matches(first, slots, groups)
    for block in range(BLOCKS):
        lanes = slice(block * LANES, (block + 1) * LANES)
        here = pl.ds(block, groups, stride=BLOCKS)
        share = jnp.log2(counts[here, :].astype(jnp.float32) / totals[0:1, :])
        merged = log_merge(first, chosen, slots, lanes, groups)
        sums = sum_merge(last, chosen, slots, lanes, groups)
        out[here, :] = BACK * (2.0 * share - merged - jnp.log2(sums))


def item_base_kernel(axis, devices, slots, middles, *refs):
    given = (1 + middles) * devices
    counts, item_total, user_total, out, numbers, all_packs = refs[given:]
    packs = [
        in_order(axis, devices, refs[step * devices : (step + 1) * devices], all_packs.at[step])
        for step in range(1 + middles)
    ]
    groups = counts.shape[0] // BLOCKS
    chosen = cluster_matches(packs[0], slots, groups)
    for index, mask in enumerate(mask for group in chosen for mask in group):
        numbers[index] = jnp.where(mask, 1.0, 0.0)
    for block in range(BLOCKS):
        lanes = slice(block * LANES, (block + 1) * LANES)
        here = pl.ds(block, groups, stride=BLOCKS)
        share = jnp.log2(counts[here, :].astype(jnp.float32) / item_total[0:1, :])
        base = (2 + middles) * share + jnp.log2(user_total[0:1, :])
        base = base - log_merge(packs[0], chosen, slots, lanes, groups)
        for step in range(middles):
            base = base - jnp.log2(sum_merge(packs[1 + step], chosen, slots, lanes, groups))
        out[here, :] = base


def item_out_kernel(axis, devices, slots, *refs):
    base, numbers, out, packs_here = refs[devices:]
    packs = in_order(axis, devices, refs[:devices], packs_here)
    groups = base.shape[0] // BLOCKS
    chosen = load_masks(numbers, devices, slots)
    for block in range(BLOCKS):
        lanes = slice(block * LANES, (block + 1) * LANES)
        here = pl.ds(block, groups, stride=BLOCKS)
        sums = sum_merge(packs, chosen, slots, lanes, groups)
        out[here, :] = BACK * (base[here, :] - jnp.log2(sums))


def paired(devices):
    return devices & (devices - 1) == 0


def partner(me, step, devices):
    if paired(devices):
        return jnp.bitwise_xor(me, step)
    return lax.rem(me + devices - step, devices)


def exchange(pack, axis, devices):
    packs = [pack]
    for step in range(1, devices):
        if paired(devices):
            route = [(device, device ^ step) for device in range(devices)]
        else:
            route = [(device, (device + step) % devices) for device in range(devices)]
        packs.append(keep(lax.ppermute(pack, axis, route)))
    return packs


def call(kernel, outs, operands, specs=None, scratch=(), **params):
    return pl.pallas_call(
        kernel,
        out_shape=outs,
        in_specs=specs or [HERE] * len(operands),
        out_specs=jax.tree.map(lambda _: HERE, outs, is_leaf=lambda leaf: not isinstance(leaf, list)),
        scratch_shapes=list(scratch),
        compiler_params=pltpu.CompilerParams(vmem_limit_bytes=16 << 20),
        **params,
    )(*operands)


def bind(kernel, *fixed):
    return lambda *refs: kernel(*fixed, *refs)


def make_body(n_user, n_item):
    def body(user_emb, item_emb, user_count, item_count, tiles, tile_count):
        slots = tiles.shape[2]
        tall = (slots, CLUSTER, CLUSTER)
        vectors = near(PACK)
        splat = near((ROWS, LANES))
        user_counts = user_count.reshape(-1, LANES)
        item_counts = item_count.reshape(-1, LANES)
        gathered = near((slots, CLUSTER, user_emb.shape[1]), user_emb.dtype)

        small = pltpu.SMEM((2, slots), jnp.int32)
        far_tiles = jnp.transpose(tiles, (0, 1, 3, 2)).reshape(2, slots)
        pack, users, items = call(
            bind(first_kernel, (n_user, n_item)),
            [vectors, gathered, gathered],
            (
                away(far_tiles), tile_count, away(user_emb), away(item_emb), away(item_counts),
            ),
            [FAR, SCALARS, FAR, FAR, FAR],
            [
                small,
                near(item_counts.shape, jnp.int32),
                near((CLUSTER, CLUSTER)),
                pltpu.SemaphoreType.DMA((2,)),
                pltpu.SemaphoreType.DMA((slots, 2)),
            ],
        )
        first_packs = exchange(pack, "item", n_item)
        table, user_here, item_here, user_ids, item_ids, notes, active = call(
            setup_kernel,
            [near(tall), vectors, vectors, splat, splat, vectors, vectors],
            (
                away(far_tiles), tile_count, keep(users), keep(items),
                away(user_counts), away(item_counts),
            ),
            [FAR, SCALARS, HERE, HERE, FAR, FAR],
            [
                small,
                near(user_counts.shape, jnp.int32),
                near(item_counts.shape, jnp.int32),
                pltpu.SemaphoreType.DMA((3,)),
            ],
        )
        pack, terms, tops, user_masks, item_total = call(
            bind(second_kernel, n_item),
            [vectors, near(tall), vectors, near((n_item * slots, ROWS, LANES)), splat],
            (*first_packs, keep(table), user_ids, user_here, notes, active),
            scratch=[near(PACK)],
        )
        terms = keep(terms)
        second_packs = exchange(pack, "user", n_user)
        pack, factor, item_masks, user_total = call(
            bind(third_kernel, n_user),
            [vectors, vectors, near((n_user * slots, ROWS, LANES)), splat],
            (*second_packs, terms, tops, item_ids, item_here, item_total),
        )
        item_packs = [second_packs]
        for iteration in range(1, ITERS):
            user_packs = exchange(pack, "item", n_item)
            (pack,) = call(
                bind(user_kernel, n_item),
                [vectors],
                (*user_packs, terms, user_masks, user_here, user_total, factor),
                scratch=[near(PACK)],
            )
            item_packs.append(exchange(pack, "user", n_user))
            if iteration < ITERS - 1:
                pack, factor = call(
                    bind(item_kernel, n_user),
                    [vectors, vectors],
                    (*item_packs[-1], terms, item_masks, item_here, item_total, factor),
                )
        user_values = call(
            bind(user_out_kernel, "item", n_item, slots),
            jax.ShapeDtypeStruct(user_counts.shape, jnp.float32),
            (*first_packs, *user_packs, user_counts, user_total),
            scratch=[near((n_item, *PACK)), near((n_item, *PACK))],
        )
        middles = ITERS - 2
        groups = item_counts.shape[0] // BLOCKS
        base, numbers = call(
            bind(item_base_kernel, "user", n_user, slots, middles),
            [near(item_counts.shape), near((n_user * slots, groups, LANES))],
            (*(pack for packs in item_packs[:-1] for pack in packs), item_counts, item_total, user_total),
            scratch=[near((1 + middles, n_user, *PACK))],
        )
        item_values = call(
            bind(item_out_kernel, "user", n_user, slots),
            jax.ShapeDtypeStruct(item_counts.shape, jnp.float32),
            (*item_packs[-1], base, numbers),
            scratch=[near((n_user, *PACK))],
        )
        return user_values.reshape(-1), item_values.reshape(-1)

    return body


def solution(mesh):
    in_specs = (
        P(("region", "user"), None),
        P(("region", "item"), None),
        P(("region", "user")),
        P(("region", "item")),
        P(("region", "user"), "item", None, None),
        P(("region", "user"), "item"),
    )
    out_specs = (P(("region", "user")), P(("region", "item")))
    return jax.shard_map(
        make_body(mesh.shape["user"], mesh.shape["item"]),
        mesh=mesh,
        in_specs=in_specs,
        out_specs=out_specs,
        check_vma=False,
    )
```

```python
import math

import jax
import jax.numpy as jnp
from jax import lax
from jax.experimental import pallas as pl
from jax.experimental.pallas import tpu as pltpu
from jax.sharding import PartitionSpec as P

CLUSTER = 512
LANES = 128
BLOCKS = CLUSTER // LANES
ROWS = 8
ITERS = 3
entropy = 0.25
lowest = -1e30
INTO = math.log2(math.e) / entropy
BACK = entropy * math.log(2.0)

HERE = pl.BlockSpec(memory_space=pltpu.VMEM)
SCALARS = pl.BlockSpec(memory_space=pltpu.SMEM)
FAR = pl.BlockSpec(memory_space=pltpu.HBM)
PACK = (ROWS, CLUSTER)


def near(shape, dtype=jnp.float32):
    return pltpu.VMEM(shape, dtype)


def keep(array):
    return pltpu.with_memory_space_constraint(array, pltpu.VMEM)


def away(array):
    return pltpu.with_memory_space_constraint(array, pltpu.HBM)


def note_at(slots, number):
    row = slots + number // BLOCKS
    lane = number % BLOCKS * LANES
    return slice(row, row + 1), slice(lane, lane + LANES)


def wide(block):
    return jnp.concatenate([block] * BLOCKS, axis=1)


def total_of(counts):
    total = jnp.sum(jnp.sum(counts.astype(jnp.float32), axis=0, keepdims=True), axis=1, keepdims=True)
    return jnp.broadcast_to(total, (1, LANES))


def write_notes(pack, tiles, which, counts):
    slots = tiles.shape[1]
    pack[slots:, :] = jnp.zeros((ROWS - slots, CLUSTER), jnp.float32)
    for slot in range(slots):
        number = jnp.full((1, LANES), tiles[which, slot], jnp.int32)
        pack[note_at(slots, slot)] = number.astype(jnp.float32)
    pack[note_at(slots, slots)] = total_of(counts)


def staggered(slots, raise_top, add_mass):
    top = raise_top(0)
    for slot in range(1, slots):
        later = raise_top(slot)
        add_mass(slot - 1, top)
        top = later
    add_mass(slots - 1, top)


def first_kernel(
    devices, far_tiles, filled, user_emb, item_emb, far_count, pack, users, items,
    tiles, item_count, scores, small_sems, sems,
):
    slots = tiles.shape[1]
    groups = user_emb.shape[0] // CLUSTER
    small = [
        pltpu.make_async_copy(source, target, small_sems.at[index])
        for index, (source, target) in enumerate(
            ((far_tiles, tiles), (far_count, item_count))
        )
    ]
    for copy in small:
        copy.start()

    def fetch(slot, groups_here):
        pair = []
        for which, (table, into) in enumerate(((user_emb, users), (item_emb, items))):
            start = pl.multiple_of(groups_here[which] * CLUSTER, CLUSTER)
            copy = pltpu.make_async_copy(
                table.at[pl.ds(start, CLUSTER)], into.at[slot], sems.at[slot, which]
            )
            copy.start()
            pair.append(copy)
        return pair

    n_user, n_item = devices
    fixed = min(groups // n_user, groups // n_item, slots)
    row, column = lax.axis_index("user"), lax.axis_index("item")
    copies = [
        fetch(slot, [lax.rem(place * fixed + slot, groups) for place in (column, row)])
        for slot in range(fixed)
    ]
    for copy in small:
        copy.wait()
    for slot in range(fixed, slots):
        copies.append(fetch(slot, [tiles[which, slot] for which in range(2)]))
    write_notes(pack, tiles, 0, item_count[...])
    early = max(1, 3 * fixed // 4)

    def raise_top(slot):
        if slot in (0, early):
            for pair in copies[:early] if slot == 0 else copies[early:]:
                for copy in pair:
                    copy.wait()
        user_block = users[slot]
        top = jnp.full((8, CLUSTER), lowest, jnp.float32)
        for block in range(BLOCKS):
            rows = slice(block * LANES, (block + 1) * LANES)
            part = lax.dot_general(
                items[slot, rows, :], user_block, (((1,), (1,)), ((), ())),
                preferred_element_type=jnp.float32,
            ) * INTO
            scores[slot, rows, :] = part
            top = jnp.maximum(top, jnp.max(part.reshape(LANES // 8, 8, CLUSTER), axis=0))
        return jnp.max(top, axis=0, keepdims=True)

    def add_mass(slot, top):
        mass = jnp.zeros((8, CLUSTER), jnp.float32)
        for block in range(BLOCKS):
            rows = slice(block * LANES, (block + 1) * LANES)
            terms = jnp.exp2(scores[slot, rows, :] - top)
            mass += jnp.sum(terms.reshape(LANES // 8, 8, CLUSTER), axis=0)
        log_mass = top + jnp.log2(jnp.sum(mass, axis=0, keepdims=True))
        pack[slot : slot + 1, :] = jnp.where(filled[0, 0] > slot, log_mass, lowest)

    staggered(slots, raise_top, add_mass)


def setup_kernel(
    far_tiles, filled, users, items, far_users, far_items,
    table, user_here, item_here, user_ids, item_ids, notes, active,
    tiles, user_count, item_count, sems,
):
    slots = tiles.shape[1]
    copies = [
        pltpu.make_async_copy(source, target, sems.at[index])
        for index, (source, target) in enumerate(
            (
                (far_tiles, tiles),
                (far_users, user_count),
                (far_items, item_count),
            )
        )
    ]
    for copy in copies:
        copy.start()
    for slot in range(slots):
        item_block = items[slot]
        for block in range(BLOCKS):
            rows = slice(block * LANES, (block + 1) * LANES)
            table[slot, rows, :] = lax.dot_general(
                users[slot, rows, :], item_block, (((1,), (1,)), ((), ())),
                preferred_element_type=jnp.float32,
            ) * INTO
    for copy in copies:
        copy.wait()
    place = lax.broadcasted_iota(jnp.int32, (ROWS, LANES), 0)
    on = jnp.where(place < filled[0, 0], 1.0, 0.0)
    active[...] = wide(on)
    for which, (counts, here, ids) in enumerate(
        ((user_count, user_here, user_ids), (item_count, item_here, item_ids))
    ):
        numbers = jnp.full((ROWS, LANES), -1, jnp.int32)
        here[...] = jnp.ones(PACK, jnp.float32)
        for slot in range(slots):
            group = tiles[which, slot]
            numbers = jnp.where(place == slot, group, numbers)
            for block in range(BLOCKS):
                here[slot : slot + 1, block * LANES : (block + 1) * LANES] = counts[
                    pl.ds(group * BLOCKS + block, 1), :
                ].astype(jnp.float32)
        ids[...] = numbers.astype(jnp.float32)
    notes[...] = jnp.zeros(PACK, jnp.float32)
    write_notes(notes, tiles, 1, user_count[...])


def matches(packs, ids, slots):
    return [
        [ids == pack[note_at(slots, slot)] for slot in range(slots)] for pack in packs
    ]


def log_merge(packs, chosen, slots, lanes, rows):
    width = lanes.stop - lanes.start
    spread = wide if width == CLUSTER else (lambda mask: mask)
    top = jnp.full((rows, width), lowest, jnp.float32)
    for pack, masks in zip(packs, chosen):
        for slot in range(slots):
            part = jnp.where(spread(masks[slot]), pack[slot : slot + 1, lanes], lowest)
            top = jnp.maximum(top, part)
    mass = jnp.zeros((rows, width), jnp.float32)
    for pack, masks in zip(packs, chosen):
        for slot in range(slots):
            part = jnp.exp2(pack[slot : slot + 1, lanes] - top)
            mass += jnp.where(spread(masks[slot]), part, 0.0)
    return top + jnp.log2(jnp.where(mass > 0.0, mass, 1.0))


def sum_merge(packs, chosen, slots, lanes, rows):
    width = lanes.stop - lanes.start
    spread = wide if width == CLUSTER else (lambda mask: mask)
    total = jnp.zeros((rows, width), jnp.float32)
    for pack, masks in zip(packs, chosen):
        for slot in range(slots):
            total += jnp.where(spread(masks[slot]), pack[slot : slot + 1, lanes], 0.0)
    return total


def total_in(packs, slots):
    total = packs[0][note_at(slots, slots)]
    for pack in packs[1:]:
        total = total + pack[note_at(slots, slots)]
    return total


def store_masks(masks, chosen):
    for index, mask in enumerate(mask for group in chosen for mask in group):
        masks[index] = jnp.where(mask, 1.0, 0.0)


def load_masks(masks, devices, slots):
    return [
        [masks[device * slots + slot] > 0.0 for slot in range(slots)] for device in range(devices)
    ]


def down_rows(vector, slot, block):
    row = vector[slot : slot + 1, block * LANES : (block + 1) * LANES]
    return jnp.broadcast_to(row, (LANES, LANES)).T


EVERY = slice(0, CLUSTER)


def second_kernel(devices, *refs):
    packs = refs[:devices]
    table, ids, counts, notes, active, pack, terms, tops, masks, totals, potential = refs[devices:]
    slots = table.shape[0]
    chosen = matches(packs, ids[...], slots)
    store_masks(masks, chosen)
    totals[...] = jnp.broadcast_to(total_in(packs, slots), totals.shape)
    potential[...] = jnp.log2(counts[...]) - log_merge(packs, chosen, slots, EVERY, ROWS)
    pack[...] = notes[...]
    tops[...] = jnp.full(PACK, lowest, jnp.float32)

    def raise_top(slot):
        top = jnp.full((8, CLUSTER), lowest, jnp.float32)
        for block in range(BLOCKS):
            rows = slice(block * LANES, (block + 1) * LANES)
            part = table[slot, rows, :] + wide(down_rows(potential, slot, block))
            terms[slot, rows, :] = part
            top = jnp.maximum(top, jnp.max(part.reshape(LANES // 8, 8, CLUSTER), axis=0))
        return jnp.max(top, axis=0, keepdims=True)

    def add_mass(slot, top):
        mass = jnp.zeros((8, CLUSTER), jnp.float32)
        for block in range(BLOCKS):
            rows = slice(block * LANES, (block + 1) * LANES)
            part = jnp.exp2(terms[slot, rows, :] - top)
            terms[slot, rows, :] = part
            mass += jnp.sum(part.reshape(LANES // 8, 8, CLUSTER), axis=0)
        log_mass = top + jnp.log2(jnp.sum(mass, axis=0, keepdims=True))
        on = active[slot : slot + 1, :] > 0.0
        pack[slot : slot + 1, :] = jnp.where(on, log_mass, lowest)
        tops[slot : slot + 1, :] = jnp.where(on, top, lowest)

    staggered(slots, raise_top, add_mass)


def row_sums(terms, factor, pack):
    slots = terms.shape[0]
    pack[...] = jnp.zeros(PACK, jnp.float32)
    for slot in range(slots):
        for block in range(BLOCKS):
            rows = slice(block * LANES, (block + 1) * LANES)
            part = terms[slot, rows, 0:LANES] * factor[slot : slot + 1, 0:LANES]
            for other in range(1, BLOCKS):
                lanes = slice(other * LANES, (other + 1) * LANES)
                part += terms[slot, rows, lanes] * factor[slot : slot + 1, lanes]
            pack[slot : slot + 1, rows] = jnp.sum(part.T, axis=0, keepdims=True)


def column_sums(terms, factor, scale, pack):
    slots = terms.shape[0]
    pack[...] = jnp.zeros(PACK, jnp.float32)
    for slot in range(slots):
        mass = jnp.zeros((8, CLUSTER), jnp.float32)
        for block in range(BLOCKS):
            rows = slice(block * LANES, (block + 1) * LANES)
            part = terms[slot, rows, :] * wide(down_rows(factor, slot, block))
            mass += jnp.sum(part.reshape(LANES // 8, 8, CLUSTER), axis=0)
        pack[slot : slot + 1, :] = jnp.sum(mass, axis=0, keepdims=True) * scale[slot : slot + 1, :]


def third_kernel(devices, *refs):
    packs = refs[:devices]
    terms, tops, ids, counts, item_total, pack, factor, masks, totals = refs[devices:]
    slots = terms.shape[0]
    chosen = matches(packs, ids[...], slots)
    store_masks(masks, chosen)
    totals[...] = jnp.broadcast_to(total_in(packs, slots), totals.shape)
    log_share = jnp.log2(counts[...] / wide(item_total[...]))
    merged = log_merge(packs, chosen, slots, EVERY, ROWS)
    factor[...] = jnp.exp2(tops[...] + (log_share - merged))
    row_sums(terms, factor, pack)


def user_kernel(devices, *refs):
    packs = refs[:devices]
    terms, masks, counts, totals, scale, pack, factor = refs[devices:]
    slots = terms.shape[0]
    sums = sum_merge(packs, load_masks(masks, devices, slots), slots, EVERY, ROWS)
    factor[...] = counts[...] / (wide(totals[...]) * jnp.where(sums > 0.0, sums, 1.0))
    column_sums(terms, factor, scale, pack)


def item_kernel(devices, *refs):
    packs = refs[:devices]
    terms, masks, counts, totals, old, pack, factor = refs[devices:]
    slots = terms.shape[0]
    sums = sum_merge(packs, load_masks(masks, devices, slots), slots, EVERY, ROWS)
    share = counts[...] / (wide(totals[...]) * jnp.where(sums > 0.0, sums, 1.0))
    factor[...] = old[...] * share
    row_sums(terms, factor, pack)


def in_order(axis, devices, packs, ordered):
    me = lax.axis_index(axis)
    for step in range(devices):
        ordered[partner(me, step, devices)] = packs[step][...]
    return [ordered.at[device] for device in range(devices)]


def cluster_matches(packs, slots, groups):
    numbers = lax.broadcasted_iota(jnp.int32, (groups, LANES), 0).astype(jnp.float32)
    return matches(packs, numbers, slots)


def user_out_kernel(axis, devices, slots, *refs):
    counts, totals, out, first_packs, last_packs = refs[2 * devices :]
    first = in_order(axis, devices, refs[:devices], first_packs)
    last = in_order(axis, devices, refs[devices : 2 * devices], last_packs)
    groups = counts.shape[0] // BLOCKS
    chosen = cluster_matches(first, slots, groups)
    for block in range(BLOCKS):
        lanes = slice(block * LANES, (block + 1) * LANES)
        here = pl.ds(block, groups, stride=BLOCKS)
        share = jnp.log2(counts[here, :].astype(jnp.float32) / totals[0:1, :])
        merged = log_merge(first, chosen, slots, lanes, groups)
        sums = sum_merge(last, chosen, slots, lanes, groups)
        out[here, :] = BACK * (2.0 * share - merged - jnp.log2(sums))


def item_base_kernel(axis, devices, slots, middles, *refs):
    given = (1 + middles) * devices
    counts, item_total, user_total, out, numbers, all_packs = refs[given:]
    packs = [
        in_order(axis, devices, refs[step * devices : (step + 1) * devices], all_packs.at[step])
        for step in range(1 + middles)
    ]
    groups = counts.shape[0] // BLOCKS
    chosen = cluster_matches(packs[0], slots, groups)
    for index, mask in enumerate(mask for group in chosen for mask in group):
        numbers[index] = jnp.where(mask, 1.0, 0.0)
    for block in range(BLOCKS):
        lanes = slice(block * LANES, (block + 1) * LANES)
        here = pl.ds(block, groups, stride=BLOCKS)
        share = jnp.log2(counts[here, :].astype(jnp.float32) / item_total[0:1, :])
        base = (2 + middles) * share + jnp.log2(user_total[0:1, :])
        base = base - log_merge(packs[0], chosen, slots, lanes, groups)
        for step in range(middles):
            base = base - jnp.log2(sum_merge(packs[1 + step], chosen, slots, lanes, groups))
        out[here, :] = base


def item_out_kernel(axis, devices, slots, *refs):
    base, numbers, out, packs_here = refs[devices:]
    packs = in_order(axis, devices, refs[:devices], packs_here)
    groups = base.shape[0] // BLOCKS
    chosen = load_masks(numbers, devices, slots)
    for block in range(BLOCKS):
        lanes = slice(block * LANES, (block + 1) * LANES)
        here = pl.ds(block, groups, stride=BLOCKS)
        sums = sum_merge(packs, chosen, slots, lanes, groups)
        out[here, :] = BACK * (base[here, :] - jnp.log2(sums))


def paired(devices):
    return devices & (devices - 1) == 0


def partner(me, step, devices):
    if paired(devices):
        return jnp.bitwise_xor(me, step)
    return lax.rem(me + devices - step, devices)


def exchange(pack, axis, devices):
    packs = [pack]
    for step in range(1, devices):
        if paired(devices):
            route = [(device, device ^ step) for device in range(devices)]
        else:
            route = [(device, (device + step) % devices) for device in range(devices)]
        packs.append(keep(lax.ppermute(pack, axis, route)))
    return packs


def call(kernel, outs, operands, specs=None, scratch=(), **params):
    return pl.pallas_call(
        kernel,
        out_shape=outs,
        in_specs=specs or [HERE] * len(operands),
        out_specs=jax.tree.map(lambda _: HERE, outs, is_leaf=lambda leaf: not isinstance(leaf, list)),
        scratch_shapes=list(scratch),
        compiler_params=pltpu.CompilerParams(vmem_limit_bytes=16 << 20),
        **params,
    )(*operands)


def bind(kernel, *fixed):
    return lambda *refs: kernel(*fixed, *refs)


def make_body(n_user, n_item):
    def body(user_emb, item_emb, user_count, item_count, tiles, tile_count):
        slots = tiles.shape[2]
        tall = (slots, CLUSTER, CLUSTER)
        vectors = near(PACK)
        splat = near((ROWS, LANES))
        user_counts = user_count.reshape(-1, LANES)
        item_counts = item_count.reshape(-1, LANES)
        gathered = near((slots, CLUSTER, user_emb.shape[1]), user_emb.dtype)

        small = pltpu.SMEM((2, slots), jnp.int32)
        far_tiles = jnp.transpose(tiles, (0, 1, 3, 2)).reshape(2, slots)
        pack, users, items = call(
            bind(first_kernel, (n_user, n_item)),
            [vectors, gathered, gathered],
            (
                away(far_tiles), tile_count, away(user_emb), away(item_emb), away(item_counts),
            ),
            [FAR, SCALARS, FAR, FAR, FAR],
            [
                small,
                near(item_counts.shape, jnp.int32),
                near(tall),
                pltpu.SemaphoreType.DMA((2,)),
                pltpu.SemaphoreType.DMA((slots, 2)),
            ],
        )
        first_packs = exchange(pack, "item", n_item)
        table, user_here, item_here, user_ids, item_ids, notes, active = call(
            setup_kernel,
            [near(tall), vectors, vectors, splat, splat, vectors, vectors],
            (
                away(far_tiles), tile_count, keep(users), keep(items),
                away(user_counts), away(item_counts),
            ),
            [FAR, SCALARS, HERE, HERE, FAR, FAR],
            [
                small,
                near(user_counts.shape, jnp.int32),
                near(item_counts.shape, jnp.int32),
                pltpu.SemaphoreType.DMA((3,)),
            ],
        )
        pack, terms, tops, user_masks, item_total = call(
            bind(second_kernel, n_item),
            [vectors, near(tall), vectors, near((n_item * slots, ROWS, LANES)), splat],
            (*first_packs, keep(table), user_ids, user_here, notes, active),
            scratch=[near(PACK)],
        )
        terms = keep(terms)
        second_packs = exchange(pack, "user", n_user)
        pack, factor, item_masks, user_total = call(
            bind(third_kernel, n_user),
            [vectors, vectors, near((n_user * slots, ROWS, LANES)), splat],
            (*second_packs, terms, tops, item_ids, item_here, item_total),
        )
        item_packs = [second_packs]
        for iteration in range(1, ITERS):
            user_packs = exchange(pack, "item", n_item)
            (pack,) = call(
                bind(user_kernel, n_item),
                [vectors],
                (*user_packs, terms, user_masks, user_here, user_total, factor),
                scratch=[near(PACK)],
            )
            item_packs.append(exchange(pack, "user", n_user))
            if iteration < ITERS - 1:
                pack, factor = call(
                    bind(item_kernel, n_user),
                    [vectors, vectors],
                    (*item_packs[-1], terms, item_masks, item_here, item_total, factor),
                )
        user_values = call(
            bind(user_out_kernel, "item", n_item, slots),
            jax.ShapeDtypeStruct(user_counts.shape, jnp.float32),
            (*first_packs, *user_packs, user_counts, user_total),
            scratch=[near((n_item, *PACK)), near((n_item, *PACK))],
        )
        middles = ITERS - 2
        groups = item_counts.shape[0] // BLOCKS
        base, numbers = call(
            bind(item_base_kernel, "user", n_user, slots, middles),
            [near(item_counts.shape), near((n_user * slots, groups, LANES))],
            (*(pack for packs in item_packs[:-1] for pack in packs), item_counts, item_total, user_total),
            scratch=[near((1 + middles, n_user, *PACK))],
        )
        item_values = call(
            bind(item_out_kernel, "user", n_user, slots),
            jax.ShapeDtypeStruct(item_counts.shape, jnp.float32),
            (*item_packs[-1], base, numbers),
            scratch=[near((n_user, *PACK))],
        )
        return user_values.reshape(-1), item_values.reshape(-1)

    return body


def solution(mesh):
    in_specs = (
        P(("region", "user"), None),
        P(("region", "item"), None),
        P(("region", "user")),
        P(("region", "item")),
        P(("region", "user"), "item", None, None),
        P(("region", "user"), "item"),
    )
    out_specs = (P(("region", "user")), P(("region", "item")))
    return jax.shard_map(
        make_body(mesh.shape["user"], mesh.shape["item"]),
        mesh=mesh,
        in_specs=in_specs,
        out_specs=out_specs,
        check_vma=False,
    )
```

```python
import math

import jax
import jax.numpy as jnp
from jax import lax
from jax.experimental import pallas as pl
from jax.experimental.pallas import tpu as pltpu
from jax.sharding import PartitionSpec as P

CLUSTER = 512
LANES = 128
BLOCKS = CLUSTER // LANES
ROWS = 8
ITERS = 3
entropy = 0.25
lowest = -1e30
INTO = math.log2(math.e) / entropy
BACK = entropy * math.log(2.0)

HERE = pl.BlockSpec(memory_space=pltpu.VMEM)
SCALARS = pl.BlockSpec(memory_space=pltpu.SMEM)
FAR = pl.BlockSpec(memory_space=pltpu.HBM)
VECTORS = (ROWS, CLUSTER)
EVERY = range(BLOCKS)


def near(shape, dtype=jnp.float32):
    return pltpu.VMEM(shape, dtype)


def keep(array):
    return pltpu.with_memory_space_constraint(array, pltpu.VMEM)


def away(array):
    return pltpu.with_memory_space_constraint(array, pltpu.HBM)


def fixed_slots(groups, n_user, n_item, slots):
    return min(groups // n_user, groups // n_item, slots)


def pack_shape(slots, fixed):
    rows = slots * BLOCKS + slots - fixed + 1
    return (rows + ROWS - 1) // ROWS * ROWS, LANES


def note(slots, number):
    row = slots * BLOCKS + number
    return slice(row, row + 1)


def part_of(block):
    return slice(block * LANES, (block + 1) * LANES)


def put(pack, slot, values):
    for block in EVERY:
        row = slot * BLOCKS + block
        pack[row : row + 1, :] = values[:, part_of(block)]


def get(pack, slot, blocks):
    rows = (slot * BLOCKS + block for block in blocks)
    return jnp.concatenate([pack[row : row + 1, :] for row in rows], axis=1)


def clear_notes(pack, slots):
    rows = pack.shape[0] - slots * BLOCKS
    pack[slots * BLOCKS :, :] = jnp.zeros((rows, LANES), jnp.float32)


def wide(block):
    return jnp.concatenate([block] * BLOCKS, axis=1)


def total_of(counts):
    total = jnp.sum(jnp.sum(counts.astype(jnp.float32), axis=0, keepdims=True), axis=1, keepdims=True)
    return jnp.broadcast_to(total, (1, LANES))


def write_notes(pack, tiles, fixed, which, counts):
    slots = tiles.shape[1]
    clear_notes(pack, slots)
    for slot in range(fixed, slots):
        number = jnp.full((1, LANES), tiles[which, slot], jnp.int32)
        pack[note(slots, slot - fixed), :] = number.astype(jnp.float32)
    pack[note(slots, slots - fixed), :] = total_of(counts)


def staggered(slots, raise_top, add_mass):
    top = raise_top(0)
    for slot in range(1, slots):
        later = raise_top(slot)
        add_mass(slot - 1, top)
        top = later
    add_mass(slots - 1, top)


def first_kernel(
    devices, far_tiles, filled, user_emb, item_emb, far_count, pack, users, items,
    tiles, item_count, scores, small_sems, sems,
):
    slots = tiles.shape[1]
    groups = user_emb.shape[0] // CLUSTER
    small = [
        pltpu.make_async_copy(source, target, small_sems.at[index])
        for index, (source, target) in enumerate(
            ((far_tiles, tiles), (far_count, item_count))
        )
    ]
    for copy in small:
        copy.start()

    def fetch(slot, groups_here):
        pair = []
        for which, (table, into) in enumerate(((user_emb, users), (item_emb, items))):
            start = pl.multiple_of(groups_here[which] * CLUSTER, CLUSTER)
            copy = pltpu.make_async_copy(
                table.at[pl.ds(start, CLUSTER)], into.at[slot], sems.at[slot, which]
            )
            copy.start()
            pair.append(copy)
        return pair

    n_user, n_item = devices
    fixed = fixed_slots(groups, n_user, n_item, slots)
    row, column = lax.axis_index("user"), lax.axis_index("item")
    copies = [
        fetch(slot, [lax.rem(place * fixed + slot, groups) for place in (column, row)])
        for slot in range(fixed)
    ]
    for copy in small:
        copy.wait()
    for slot in range(fixed, slots):
        copies.append(fetch(slot, [tiles[which, slot] for which in range(2)]))
    write_notes(pack, tiles, fixed, 0, item_count[...])
    early = max(1, 3 * fixed // 4)

    def raise_top(slot):
        if slot in (0, early):
            for pair in copies[:early] if slot == 0 else copies[early:]:
                for copy in pair:
                    copy.wait()
        user_block = users[slot]
        top = jnp.full((8, CLUSTER), lowest, jnp.float32)
        for block in range(BLOCKS):
            rows = slice(block * LANES, (block + 1) * LANES)
            part = lax.dot_general(
                items[slot, rows, :], user_block, (((1,), (1,)), ((), ())),
                preferred_element_type=jnp.float32,
            ) * INTO
            scores[slot, rows, :] = part
            top = jnp.maximum(top, jnp.max(part.reshape(LANES // 8, 8, CLUSTER), axis=0))
        return jnp.max(top, axis=0, keepdims=True)

    def add_mass(slot, top):
        mass = jnp.zeros((8, CLUSTER), jnp.float32)
        for block in range(BLOCKS):
            rows = slice(block * LANES, (block + 1) * LANES)
            terms = jnp.exp2(scores[slot, rows, :] - top)
            mass += jnp.sum(terms.reshape(LANES // 8, 8, CLUSTER), axis=0)
        log_mass = top + jnp.log2(jnp.sum(mass, axis=0, keepdims=True))
        put(pack, slot, jnp.where(filled[0, 0] > slot, log_mass, lowest))

    staggered(slots, raise_top, add_mass)


def setup_kernel(
    devices, far_tiles, filled, users, items, far_users, far_items,
    table, user_here, item_here, user_ids, item_ids, notes, active,
    tiles, user_count, item_count, sems,
):
    slots = tiles.shape[1]
    copies = [
        pltpu.make_async_copy(source, target, sems.at[index])
        for index, (source, target) in enumerate(
            (
                (far_tiles, tiles),
                (far_users, user_count),
                (far_items, item_count),
            )
        )
    ]
    for copy in copies:
        copy.start()
    for slot in range(slots):
        item_block = items[slot]
        for block in range(BLOCKS):
            rows = slice(block * LANES, (block + 1) * LANES)
            table[slot, rows, :] = lax.dot_general(
                users[slot, rows, :], item_block, (((1,), (1,)), ((), ())),
                preferred_element_type=jnp.float32,
            ) * INTO
    for copy in copies:
        copy.wait()
    place = lax.broadcasted_iota(jnp.int32, (ROWS, LANES), 0)
    on = jnp.where(place < filled[0, 0], 1.0, 0.0)
    active[...] = wide(on)
    for which, (counts, here, ids) in enumerate(
        ((user_count, user_here, user_ids), (item_count, item_here, item_ids))
    ):
        numbers = jnp.full((ROWS, LANES), -1, jnp.int32)
        here[...] = jnp.ones(VECTORS, jnp.float32)
        for slot in range(slots):
            group = tiles[which, slot]
            numbers = jnp.where(place == slot, group, numbers)
            for block in range(BLOCKS):
                here[slot : slot + 1, block * LANES : (block + 1) * LANES] = counts[
                    pl.ds(group * BLOCKS + block, 1), :
                ].astype(jnp.float32)
        ids[...] = numbers
    fixed = fixed_slots(user_count.shape[0] // BLOCKS, *devices, slots)
    write_notes(notes, tiles, fixed, 1, user_count[...])


def matches(packs, owners, ids, slots, fixed, groups):
    chosen = []
    for pack, owner in zip(packs, owners):
        masks = [ids == (owner * fixed + slot) % groups for slot in range(fixed)]
        for number in range(slots - fixed):
            masks.append(ids == pack[note(slots, number), :].astype(jnp.int32))
        chosen.append(masks)
    return chosen


def across(mask, blocks):
    return jnp.concatenate([mask] * len(blocks), axis=1)


def log_merge(packs, chosen, slots, blocks, rows):
    width = len(blocks) * LANES
    top = jnp.full((rows, width), lowest, jnp.float32)
    for pack, masks in zip(packs, chosen):
        for slot in range(slots):
            part = jnp.where(across(masks[slot], blocks), get(pack, slot, blocks), lowest)
            top = jnp.maximum(top, part)
    mass = jnp.zeros((rows, width), jnp.float32)
    for pack, masks in zip(packs, chosen):
        for slot in range(slots):
            part = jnp.exp2(get(pack, slot, blocks) - top)
            mass += jnp.where(across(masks[slot], blocks), part, 0.0)
    return top + jnp.log2(jnp.where(mass > 0.0, mass, 1.0))


def sum_merge(packs, chosen, slots, blocks, rows):
    total = jnp.zeros((rows, len(blocks) * LANES), jnp.float32)
    for pack, masks in zip(packs, chosen):
        for slot in range(slots):
            total += jnp.where(across(masks[slot], blocks), get(pack, slot, blocks), 0.0)
    return total


def total_in(packs, slots, fixed):
    row = note(slots, slots - fixed)
    total = packs[0][row, :]
    for pack in packs[1:]:
        total = total + pack[row, :]
    return total


def owners_of(axis, devices):
    me = lax.axis_index(axis)
    return [partner(me, step, devices) for step in range(devices)]


def store_masks(masks, chosen):
    for index, mask in enumerate(mask for group in chosen for mask in group):
        masks[index] = jnp.where(mask, 1.0, 0.0)


def load_masks(masks, devices, slots):
    return [
        [masks[device * slots + slot] > 0.0 for slot in range(slots)] for device in range(devices)
    ]


def down_rows(vector, slot, block):
    row = vector[slot : slot + 1, block * LANES : (block + 1) * LANES]
    return jnp.broadcast_to(row, (LANES, LANES)).T


def second_kernel(axis, devices, fixed, groups, *refs):
    packs = refs[:devices]
    table, ids, counts, notes, active, pack, terms, tops, masks, totals, potential = refs[devices:]
    slots = table.shape[0]
    chosen = matches(packs, owners_of(axis, devices), ids[...], slots, fixed, groups)
    store_masks(masks, chosen)
    totals[...] = jnp.broadcast_to(total_in(packs, slots, fixed), totals.shape)
    potential[...] = jnp.log2(counts[...]) - log_merge(packs, chosen, slots, EVERY, ROWS)
    pack[...] = notes[...]
    tops[...] = jnp.full(VECTORS, lowest, jnp.float32)

    def raise_top(slot):
        top = jnp.full((8, CLUSTER), lowest, jnp.float32)
        for block in range(BLOCKS):
            rows = slice(block * LANES, (block + 1) * LANES)
            part = table[slot, rows, :] + wide(down_rows(potential, slot, block))
            terms[slot, rows, :] = part
            top = jnp.maximum(top, jnp.max(part.reshape(LANES // 8, 8, CLUSTER), axis=0))
        return jnp.max(top, axis=0, keepdims=True)

    def add_mass(slot, top):
        mass = jnp.zeros((8, CLUSTER), jnp.float32)
        for block in range(BLOCKS):
            rows = slice(block * LANES, (block + 1) * LANES)
            part = jnp.exp2(terms[slot, rows, :] - top)
            terms[slot, rows, :] = part
            mass += jnp.sum(part.reshape(LANES // 8, 8, CLUSTER), axis=0)
        log_mass = top + jnp.log2(jnp.sum(mass, axis=0, keepdims=True))
        on = active[slot : slot + 1, :] > 0.0
        put(pack, slot, jnp.where(on, log_mass, lowest))
        tops[slot : slot + 1, :] = jnp.where(on, top, lowest)

    staggered(slots, raise_top, add_mass)


def row_sums(terms, factor, pack):
    slots = terms.shape[0]
    clear_notes(pack, slots)
    for slot in range(slots):
        for block in range(BLOCKS):
            rows = slice(block * LANES, (block + 1) * LANES)
            part = terms[slot, rows, 0:LANES] * factor[slot : slot + 1, 0:LANES]
            for other in range(1, BLOCKS):
                lanes = slice(other * LANES, (other + 1) * LANES)
                part += terms[slot, rows, lanes] * factor[slot : slot + 1, lanes]
            row = slot * BLOCKS + block
            pack[row : row + 1, :] = jnp.sum(part.T, axis=0, keepdims=True)


def column_sums(terms, factor, scale, pack):
    slots = terms.shape[0]
    clear_notes(pack, slots)
    for slot in range(slots):
        mass = jnp.zeros((8, CLUSTER), jnp.float32)
        for block in range(BLOCKS):
            rows = slice(block * LANES, (block + 1) * LANES)
            part = terms[slot, rows, :] * wide(down_rows(factor, slot, block))
            mass += jnp.sum(part.reshape(LANES // 8, 8, CLUSTER), axis=0)
        put(pack, slot, jnp.sum(mass, axis=0, keepdims=True) * scale[slot : slot + 1, :])


def third_kernel(axis, devices, fixed, groups, *refs):
    packs = refs[:devices]
    terms, tops, ids, counts, item_total, pack, factor, masks, totals = refs[devices:]
    slots = terms.shape[0]
    chosen = matches(packs, owners_of(axis, devices), ids[...], slots, fixed, groups)
    store_masks(masks, chosen)
    totals[...] = jnp.broadcast_to(total_in(packs, slots, fixed), totals.shape)
    log_share = jnp.log2(counts[...] / wide(item_total[...]))
    merged = log_merge(packs, chosen, slots, EVERY, ROWS)
    factor[...] = jnp.exp2(tops[...] + (log_share - merged))
    row_sums(terms, factor, pack)


def user_kernel(devices, *refs):
    packs = refs[:devices]
    terms, masks, counts, totals, scale, pack, factor = refs[devices:]
    slots = terms.shape[0]
    sums = sum_merge(packs, load_masks(masks, devices, slots), slots, EVERY, ROWS)
    factor[...] = counts[...] / (wide(totals[...]) * jnp.where(sums > 0.0, sums, 1.0))
    column_sums(terms, factor, scale, pack)


def item_kernel(devices, *refs):
    packs = refs[:devices]
    terms, masks, counts, totals, old, pack, factor = refs[devices:]
    slots = terms.shape[0]
    sums = sum_merge(packs, load_masks(masks, devices, slots), slots, EVERY, ROWS)
    share = counts[...] / (wide(totals[...]) * jnp.where(sums > 0.0, sums, 1.0))
    factor[...] = old[...] * share
    row_sums(terms, factor, pack)


def in_order(axis, devices, packs, ordered):
    me = lax.axis_index(axis)
    for step in range(devices):
        ordered[partner(me, step, devices)] = packs[step][...]
    return [ordered.at[device] for device in range(devices)]


def cluster_matches(packs, slots, fixed, groups):
    numbers = lax.broadcasted_iota(jnp.int32, (groups, LANES), 0)
    return matches(packs, range(len(packs)), numbers, slots, fixed, groups)


def user_out_kernel(axis, devices, slots, fixed, *refs):
    counts, totals, out, first_packs, last_packs = refs[2 * devices :]
    first = in_order(axis, devices, refs[:devices], first_packs)
    last = in_order(axis, devices, refs[devices : 2 * devices], last_packs)
    groups = counts.shape[0] // BLOCKS
    chosen = cluster_matches(first, slots, fixed, groups)
    for block in range(BLOCKS):
        here = pl.ds(block, groups, stride=BLOCKS)
        share = jnp.log2(counts[here, :].astype(jnp.float32) / totals[0:1, :])
        merged = log_merge(first, chosen, slots, [block], groups)
        sums = sum_merge(last, chosen, slots, [block], groups)
        out[here, :] = BACK * (2.0 * share - merged - jnp.log2(sums))


def item_base_kernel(axis, devices, slots, fixed, middles, *refs):
    given = (1 + middles) * devices
    counts, item_total, user_total, out, numbers, all_packs = refs[given:]
    packs = [
        in_order(axis, devices, refs[step * devices : (step + 1) * devices], all_packs.at[step])
        for step in range(1 + middles)
    ]
    groups = counts.shape[0] // BLOCKS
    chosen = cluster_matches(packs[0], slots, fixed, groups)
    for index, mask in enumerate(mask for group in chosen for mask in group):
        numbers[index] = jnp.where(mask, 1.0, 0.0)
    for block in range(BLOCKS):
        here = pl.ds(block, groups, stride=BLOCKS)
        share = jnp.log2(counts[here, :].astype(jnp.float32) / item_total[0:1, :])
        base = (2 + middles) * share + jnp.log2(user_total[0:1, :])
        base = base - log_merge(packs[0], chosen, slots, [block], groups)
        for step in range(middles):
            base = base - jnp.log2(sum_merge(packs[1 + step], chosen, slots, [block], groups))
        out[here, :] = base


def item_out_kernel(axis, devices, slots, *refs):
    base, numbers, out, packs_here = refs[devices:]
    packs = in_order(axis, devices, refs[:devices], packs_here)
    groups = base.shape[0] // BLOCKS
    chosen = load_masks(numbers, devices, slots)
    for block in range(BLOCKS):
        here = pl.ds(block, groups, stride=BLOCKS)
        sums = sum_merge(packs, chosen, slots, [block], groups)
        out[here, :] = BACK * (base[here, :] - jnp.log2(sums))


def paired(devices):
    return devices & (devices - 1) == 0


def partner(me, step, devices):
    if paired(devices):
        return jnp.bitwise_xor(me, step)
    return lax.rem(me + devices - step, devices)


def exchange(pack, axis, devices):
    packs = [pack]
    for step in range(1, devices):
        if paired(devices):
            route = [(device, device ^ step) for device in range(devices)]
        else:
            route = [(device, (device + step) % devices) for device in range(devices)]
        packs.append(keep(lax.ppermute(pack, axis, route)))
    return packs


def call(kernel, outs, operands, specs=None, scratch=(), **params):
    return pl.pallas_call(
        kernel,
        out_shape=outs,
        in_specs=specs or [HERE] * len(operands),
        out_specs=jax.tree.map(lambda _: HERE, outs, is_leaf=lambda leaf: not isinstance(leaf, list)),
        scratch_shapes=list(scratch),
        compiler_params=pltpu.CompilerParams(vmem_limit_bytes=16 << 20),
        **params,
    )(*operands)


def bind(kernel, *fixed):
    return lambda *refs: kernel(*fixed, *refs)


def make_body(n_user, n_item):
    def body(user_emb, item_emb, user_count, item_count, tiles, tile_count):
        slots = tiles.shape[2]
        tall = (slots, CLUSTER, CLUSTER)
        groups = user_emb.shape[0] // CLUSTER
        fixed = fixed_slots(groups, n_user, n_item, slots)
        shape = pack_shape(slots, fixed)
        packed = near(shape)
        vectors = near(VECTORS)
        splat = near((ROWS, LANES))
        numbers = near((ROWS, LANES), jnp.int32)
        user_counts = user_count.reshape(-1, LANES)
        item_counts = item_count.reshape(-1, LANES)
        gathered = near((slots, CLUSTER, user_emb.shape[1]), user_emb.dtype)

        small = pltpu.SMEM((2, slots), jnp.int32)
        far_tiles = jnp.transpose(tiles, (0, 1, 3, 2)).reshape(2, slots)
        pack, users, items = call(
            bind(first_kernel, (n_user, n_item)),
            [packed, gathered, gathered],
            (
                away(far_tiles), tile_count, away(user_emb), away(item_emb), away(item_counts),
            ),
            [FAR, SCALARS, FAR, FAR, FAR],
            [
                small,
                near(item_counts.shape, jnp.int32),
                near(tall),
                pltpu.SemaphoreType.DMA((2,)),
                pltpu.SemaphoreType.DMA((slots, 2)),
            ],
        )
        first_packs = exchange(pack, "item", n_item)
        table, user_here, item_here, user_ids, item_ids, notes, active = call(
            bind(setup_kernel, (n_user, n_item)),
            [near(tall), vectors, vectors, numbers, numbers, packed, vectors],
            (
                away(far_tiles), tile_count, keep(users), keep(items),
                away(user_counts), away(item_counts),
            ),
            [FAR, SCALARS, HERE, HERE, FAR, FAR],
            [
                small,
                near(user_counts.shape, jnp.int32),
                near(item_counts.shape, jnp.int32),
                pltpu.SemaphoreType.DMA((3,)),
            ],
        )
        pack, terms, tops, user_masks, item_total = call(
            bind(second_kernel, "item", n_item, fixed, groups),
            [packed, near(tall), vectors, near((n_item * slots, ROWS, LANES)), splat],
            (*first_packs, keep(table), user_ids, user_here, notes, active),
            scratch=[near(VECTORS)],
        )
        terms = keep(terms)
        second_packs = exchange(pack, "user", n_user)
        pack, factor, item_masks, user_total = call(
            bind(third_kernel, "user", n_user, fixed, groups),
            [packed, vectors, near((n_user * slots, ROWS, LANES)), splat],
            (*second_packs, terms, tops, item_ids, item_here, item_total),
        )
        item_packs = [second_packs]
        for iteration in range(1, ITERS):
            user_packs = exchange(pack, "item", n_item)
            (pack,) = call(
                bind(user_kernel, n_item),
                [packed],
                (*user_packs, terms, user_masks, user_here, user_total, factor),
                scratch=[near(VECTORS)],
            )
            item_packs.append(exchange(pack, "user", n_user))
            if iteration < ITERS - 1:
                pack, factor = call(
                    bind(item_kernel, n_user),
                    [packed, vectors],
                    (*item_packs[-1], terms, item_masks, item_here, item_total, factor),
                )
        user_values = call(
            bind(user_out_kernel, "item", n_item, slots, fixed),
            jax.ShapeDtypeStruct(user_counts.shape, jnp.float32),
            (*first_packs, *user_packs, user_counts, user_total),
            scratch=[near((n_item, *shape)), near((n_item, *shape))],
        )
        middles = ITERS - 2
        base, named = call(
            bind(item_base_kernel, "user", n_user, slots, fixed, middles),
            [near(item_counts.shape), near((n_user * slots, groups, LANES))],
            (*(pack for packs in item_packs[:-1] for pack in packs), item_counts, item_total, user_total),
            scratch=[near((1 + middles, n_user, *shape))],
        )
        item_values = call(
            bind(item_out_kernel, "user", n_user, slots),
            jax.ShapeDtypeStruct(item_counts.shape, jnp.float32),
            (*item_packs[-1], base, named),
            scratch=[near((n_user, *shape))],
        )
        return user_values.reshape(-1), item_values.reshape(-1)

    return body


def solution(mesh):
    in_specs = (
        P(("region", "user"), None),
        P(("region", "item"), None),
        P(("region", "user")),
        P(("region", "item")),
        P(("region", "user"), "item", None, None),
        P(("region", "user"), "item"),
    )
    out_specs = (P(("region", "user")), P(("region", "item")))
    return jax.shard_map(
        make_body(mesh.shape["user"], mesh.shape["item"]),
        mesh=mesh,
        in_specs=in_specs,
        out_specs=out_specs,
        check_vma=False,
    )
```

```python
import functools
import math

import jax
import jax.numpy as jnp
from jax import lax
from jax.experimental import pallas as pl
from jax.experimental.pallas import tpu as pltpu
from jax.sharding import PartitionSpec as P

CLUSTER = 512
LANES = 128
BLOCKS = CLUSTER // LANES
ROWS = 8
STRIP = 32
ITERS = 3
entropy = 0.25
lowest = -1e30
INTO = math.log2(math.e) / entropy
BACK = entropy * math.log(2.0)

HERE = pl.BlockSpec(memory_space=pltpu.VMEM)
SCALARS = pl.BlockSpec(memory_space=pltpu.SMEM)
FAR = pl.BlockSpec(memory_space=pltpu.HBM)
VECTORS = (ROWS, CLUSTER)
EVERY = range(BLOCKS)


def near(shape, dtype=jnp.float32):
    return pltpu.VMEM(shape, dtype)


def keep(array):
    return pltpu.with_memory_space_constraint(array, pltpu.VMEM)


def away(array):
    return pltpu.with_memory_space_constraint(array, pltpu.HBM)


def fixed_slots(groups, n_user, n_item, slots):
    return min(groups // n_user, groups // n_item, slots)


def pack_shape(slots, fixed):
    rows = slots * BLOCKS + slots - fixed + 1
    return (rows + ROWS - 1) // ROWS * ROWS, LANES


def note(slots, number):
    row = slots * BLOCKS + number
    return slice(row, row + 1)


def part_of(block):
    return slice(block * LANES, (block + 1) * LANES)


def put(pack, slot, values):
    for block in EVERY:
        row = slot * BLOCKS + block
        pack[row : row + 1, :] = values[:, part_of(block)]


def get(pack, slot, blocks):
    rows = (slot * BLOCKS + block for block in blocks)
    return jnp.concatenate([pack[row : row + 1, :] for row in rows], axis=1)


def clear_notes(pack, slots):
    rows = pack.shape[0] - slots * BLOCKS
    pack[slots * BLOCKS :, :] = jnp.zeros((rows, LANES), jnp.float32)


def wide(block):
    return jnp.concatenate([block] * BLOCKS, axis=1)


def total_of(counts):
    total = jnp.sum(jnp.sum(counts.astype(jnp.float32), axis=0, keepdims=True), axis=1, keepdims=True)
    return jnp.broadcast_to(total, (1, LANES))


def write_notes(pack, tiles, fixed, which, counts):
    slots = tiles.shape[1]
    clear_notes(pack, slots)
    for slot in range(fixed, slots):
        number = jnp.full((1, LANES), tiles[which, slot], jnp.int32)
        pack[note(slots, slot - fixed), :] = number.astype(jnp.float32)
    pack[note(slots, slots - fixed), :] = total_of(counts)


def staggered(slots, raise_top, add_mass):
    top = raise_top(0)
    for slot in range(1, slots):
        later = raise_top(slot)
        add_mass(slot - 1, top)
        top = later
    add_mass(slots - 1, top)


def first_kernel(
    devices, far_tiles, filled, user_emb, item_emb, far_count, pack, users, items,
    tiles, item_count, small_sems, sems,
):
    slots = tiles.shape[1]
    groups = user_emb.shape[0] // CLUSTER
    small = [
        pltpu.make_async_copy(source, target, small_sems.at[index])
        for index, (source, target) in enumerate(
            ((far_tiles, tiles), (far_count, item_count))
        )
    ]
    for copy in small:
        copy.start()

    def fetch(slot, groups_here):
        pair = []
        for which, (table, into) in enumerate(((user_emb, users), (item_emb, items))):
            start = pl.multiple_of(groups_here[which] * CLUSTER, CLUSTER)
            copy = pltpu.make_async_copy(
                table.at[pl.ds(start, CLUSTER)], into.at[slot], sems.at[slot, which]
            )
            copy.start()
            pair.append(copy)
        return pair

    n_user, n_item = devices
    fixed = fixed_slots(groups, n_user, n_item, slots)
    row, column = lax.axis_index("user"), lax.axis_index("item")
    copies = [
        fetch(slot, [lax.rem(place * fixed + slot, groups) for place in (column, row)])
        for slot in range(fixed)
    ]
    for copy in small:
        copy.wait()
    for slot in range(fixed, slots):
        copies.append(fetch(slot, [tiles[which, slot] for which in range(2)]))
    write_notes(pack, tiles, fixed, 0, item_count[...])
    early = max(1, 3 * fixed // 4)

    for slot in range(slots):
        if slot in (0, early):
            for pair in copies[:early] if slot == 0 else copies[early:]:
                for copy in pair:
                    copy.wait()
        scores = lax.dot_general(
            items[slot], users[slot], (((1,), (1,)), ((), ())), preferred_element_type=jnp.float32
        ) * INTO
        tops, masses = [], []
        for row in range(0, CLUSTER, STRIP):
            part = scores[row : row + STRIP].reshape(STRIP // 8, 8, CLUSTER)
            tops.append(jnp.max(part, axis=0))
            masses.append(jnp.sum(jnp.exp2(part - tops[-1]), axis=0))
        top = jnp.max(functools.reduce(jnp.maximum, tops), axis=0, keepdims=True)
        mass = sum(mass * jnp.exp2(old - top) for mass, old in zip(masses, tops))
        log_mass = top + jnp.log2(jnp.sum(mass, axis=0, keepdims=True))
        put(pack, slot, jnp.where(filled[0, 0] > slot, log_mass, lowest))


def setup_kernel(
    devices, far_tiles, filled, users, items, far_users, far_items,
    table, user_here, item_here, user_ids, item_ids, notes, active,
    tiles, user_count, item_count, sems,
):
    slots = tiles.shape[1]
    copies = [
        pltpu.make_async_copy(source, target, sems.at[index])
        for index, (source, target) in enumerate(
            (
                (far_tiles, tiles),
                (far_users, user_count),
                (far_items, item_count),
            )
        )
    ]
    for copy in copies:
        copy.start()
    for slot in range(slots):
        item_block = items[slot]
        for block in range(BLOCKS):
            rows = slice(block * LANES, (block + 1) * LANES)
            table[slot, rows, :] = lax.dot_general(
                users[slot, rows, :], item_block, (((1,), (1,)), ((), ())),
                preferred_element_type=jnp.float32,
            ) * INTO
    for copy in copies:
        copy.wait()
    place = lax.broadcasted_iota(jnp.int32, (ROWS, LANES), 0)
    on = jnp.where(place < filled[0, 0], 1.0, 0.0)
    active[...] = wide(on)
    for which, (counts, here, ids) in enumerate(
        ((user_count, user_here, user_ids), (item_count, item_here, item_ids))
    ):
        numbers = jnp.full((ROWS, LANES), -1, jnp.int32)
        here[...] = jnp.ones(VECTORS, jnp.float32)
        for slot in range(slots):
            group = tiles[which, slot]
            numbers = jnp.where(place == slot, group, numbers)
            for block in range(BLOCKS):
                here[slot : slot + 1, block * LANES : (block + 1) * LANES] = counts[
                    pl.ds(group * BLOCKS + block, 1), :
                ].astype(jnp.float32)
        ids[...] = numbers
    fixed = fixed_slots(user_count.shape[0] // BLOCKS, *devices, slots)
    write_notes(notes, tiles, fixed, 1, user_count[...])


def matches(packs, owners, ids, slots, fixed, groups):
    chosen = []
    for pack, owner in zip(packs, owners):
        masks = [ids == (owner * fixed + slot) % groups for slot in range(fixed)]
        for number in range(slots - fixed):
            masks.append(ids == pack[note(slots, number), :].astype(jnp.int32))
        chosen.append(masks)
    return chosen


def across(mask, blocks):
    return jnp.concatenate([mask] * len(blocks), axis=1)


def log_merge(packs, chosen, slots, blocks, rows):
    width = len(blocks) * LANES
    top = jnp.full((rows, width), lowest, jnp.float32)
    for pack, masks in zip(packs, chosen):
        for slot in range(slots):
            part = jnp.where(across(masks[slot], blocks), get(pack, slot, blocks), lowest)
            top = jnp.maximum(top, part)
    mass = jnp.zeros((rows, width), jnp.float32)
    for pack, masks in zip(packs, chosen):
        for slot in range(slots):
            part = jnp.exp2(get(pack, slot, blocks) - top)
            mass += jnp.where(across(masks[slot], blocks), part, 0.0)
    return top + jnp.log2(jnp.where(mass > 0.0, mass, 1.0))


def sum_merge(packs, chosen, slots, blocks, rows):
    total = jnp.zeros((rows, len(blocks) * LANES), jnp.float32)
    for pack, masks in zip(packs, chosen):
        for slot in range(slots):
            total += jnp.where(across(masks[slot], blocks), get(pack, slot, blocks), 0.0)
    return total


def total_in(packs, slots, fixed):
    row = note(slots, slots - fixed)
    total = packs[0][row, :]
    for pack in packs[1:]:
        total = total + pack[row, :]
    return total


def owners_of(axis, devices):
    me = lax.axis_index(axis)
    return [partner(me, step, devices) for step in range(devices)]


def store_masks(masks, chosen):
    for index, mask in enumerate(mask for group in chosen for mask in group):
        masks[index] = jnp.where(mask, 1.0, 0.0)


def load_masks(masks, devices, slots):
    return [
        [masks[device * slots + slot] > 0.0 for slot in range(slots)] for device in range(devices)
    ]


def down_rows(vector, slot, block):
    row = vector[slot : slot + 1, block * LANES : (block + 1) * LANES]
    return jnp.broadcast_to(row, (LANES, LANES)).T


def second_kernel(axis, devices, fixed, groups, *refs):
    packs = refs[:devices]
    table, ids, counts, notes, active, pack, terms, tops, masks, totals, potential = refs[devices:]
    slots = table.shape[0]
    chosen = matches(packs, owners_of(axis, devices), ids[...], slots, fixed, groups)
    store_masks(masks, chosen)
    totals[...] = jnp.broadcast_to(total_in(packs, slots, fixed), totals.shape)
    potential[...] = jnp.log2(counts[...]) - log_merge(packs, chosen, slots, EVERY, ROWS)
    pack[...] = notes[...]
    tops[...] = jnp.full(VECTORS, lowest, jnp.float32)

    def raise_top(slot):
        top = jnp.full((8, CLUSTER), lowest, jnp.float32)
        for block in range(BLOCKS):
            rows = slice(block * LANES, (block + 1) * LANES)
            part = table[slot, rows, :] + wide(down_rows(potential, slot, block))
            terms[slot, rows, :] = part
            top = jnp.maximum(top, jnp.max(part.reshape(LANES // 8, 8, CLUSTER), axis=0))
        return jnp.max(top, axis=0, keepdims=True)

    def add_mass(slot, top):
        mass = jnp.zeros((8, CLUSTER), jnp.float32)
        for block in range(BLOCKS):
            rows = slice(block * LANES, (block + 1) * LANES)
            part = jnp.exp2(terms[slot, rows, :] - top)
            terms[slot, rows, :] = part
            mass += jnp.sum(part.reshape(LANES // 8, 8, CLUSTER), axis=0)
        log_mass = top + jnp.log2(jnp.sum(mass, axis=0, keepdims=True))
        on = active[slot : slot + 1, :] > 0.0
        put(pack, slot, jnp.where(on, log_mass, lowest))
        tops[slot : slot + 1, :] = jnp.where(on, top, lowest)

    staggered(slots, raise_top, add_mass)


def row_sums(terms, factor, pack):
    slots = terms.shape[0]
    clear_notes(pack, slots)
    for slot in range(slots):
        for block in range(BLOCKS):
            rows = slice(block * LANES, (block + 1) * LANES)
            part = terms[slot, rows, 0:LANES] * factor[slot : slot + 1, 0:LANES]
            for other in range(1, BLOCKS):
                lanes = slice(other * LANES, (other + 1) * LANES)
                part += terms[slot, rows, lanes] * factor[slot : slot + 1, lanes]
            row = slot * BLOCKS + block
            pack[row : row + 1, :] = jnp.sum(part.T, axis=0, keepdims=True)


def column_sums(terms, factor, scale, pack):
    slots = terms.shape[0]
    clear_notes(pack, slots)
    for slot in range(slots):
        mass = jnp.zeros((8, CLUSTER), jnp.float32)
        for block in range(BLOCKS):
            rows = slice(block * LANES, (block + 1) * LANES)
            part = terms[slot, rows, :] * wide(down_rows(factor, slot, block))
            mass += jnp.sum(part.reshape(LANES // 8, 8, CLUSTER), axis=0)
        put(pack, slot, jnp.sum(mass, axis=0, keepdims=True) * scale[slot : slot + 1, :])


def third_kernel(axis, devices, fixed, groups, *refs):
    packs = refs[:devices]
    terms, tops, ids, counts, item_total, pack, factor, masks, totals = refs[devices:]
    slots = terms.shape[0]
    chosen = matches(packs, owners_of(axis, devices), ids[...], slots, fixed, groups)
    store_masks(masks, chosen)
    totals[...] = jnp.broadcast_to(total_in(packs, slots, fixed), totals.shape)
    log_share = jnp.log2(counts[...] / wide(item_total[...]))
    merged = log_merge(packs, chosen, slots, EVERY, ROWS)
    factor[...] = jnp.exp2(tops[...] + (log_share - merged))
    row_sums(terms, factor, pack)


def user_kernel(devices, *refs):
    packs = refs[:devices]
    terms, masks, counts, totals, scale, pack, factor = refs[devices:]
    slots = terms.shape[0]
    sums = sum_merge(packs, load_masks(masks, devices, slots), slots, EVERY, ROWS)
    factor[...] = counts[...] / (wide(totals[...]) * jnp.where(sums > 0.0, sums, 1.0))
    column_sums(terms, factor, scale, pack)


def item_kernel(devices, *refs):
    packs = refs[:devices]
    terms, masks, counts, totals, old, pack, factor = refs[devices:]
    slots = terms.shape[0]
    sums = sum_merge(packs, load_masks(masks, devices, slots), slots, EVERY, ROWS)
    share = counts[...] / (wide(totals[...]) * jnp.where(sums > 0.0, sums, 1.0))
    factor[...] = old[...] * share
    row_sums(terms, factor, pack)


def in_order(axis, devices, packs, ordered):
    me = lax.axis_index(axis)
    for step in range(devices):
        ordered[partner(me, step, devices)] = packs[step][...]
    return [ordered.at[device] for device in range(devices)]


def cluster_matches(packs, slots, fixed, groups):
    numbers = lax.broadcasted_iota(jnp.int32, (groups, LANES), 0)
    return matches(packs, range(len(packs)), numbers, slots, fixed, groups)


def user_out_kernel(axis, devices, slots, fixed, *refs):
    counts, totals, out, first_packs, last_packs = refs[2 * devices :]
    first = in_order(axis, devices, refs[:devices], first_packs)
    last = in_order(axis, devices, refs[devices : 2 * devices], last_packs)
    groups = counts.shape[0] // BLOCKS
    chosen = cluster_matches(first, slots, fixed, groups)
    for block in range(BLOCKS):
        here = pl.ds(block, groups, stride=BLOCKS)
        share = jnp.log2(counts[here, :].astype(jnp.float32) / totals[0:1, :])
        merged = log_merge(first, chosen, slots, [block], groups)
        sums = sum_merge(last, chosen, slots, [block], groups)
        out[here, :] = BACK * (2.0 * share - merged - jnp.log2(sums))


def item_base_kernel(axis, devices, slots, fixed, middles, *refs):
    given = (1 + middles) * devices
    counts, item_total, user_total, out, numbers, all_packs = refs[given:]
    packs = [
        in_order(axis, devices, refs[step * devices : (step + 1) * devices], all_packs.at[step])
        for step in range(1 + middles)
    ]
    groups = counts.shape[0] // BLOCKS
    chosen = cluster_matches(packs[0], slots, fixed, groups)
    for index, mask in enumerate(mask for group in chosen for mask in group):
        numbers[index] = jnp.where(mask, 1.0, 0.0)
    for block in range(BLOCKS):
        here = pl.ds(block, groups, stride=BLOCKS)
        share = jnp.log2(counts[here, :].astype(jnp.float32) / item_total[0:1, :])
        base = (2 + middles) * share + jnp.log2(user_total[0:1, :])
        base = base - log_merge(packs[0], chosen, slots, [block], groups)
        for step in range(middles):
            base = base - jnp.log2(sum_merge(packs[1 + step], chosen, slots, [block], groups))
        out[here, :] = base


def item_out_kernel(axis, devices, slots, *refs):
    base, numbers, out, packs_here = refs[devices:]
    packs = in_order(axis, devices, refs[:devices], packs_here)
    groups = base.shape[0] // BLOCKS
    chosen = load_masks(numbers, devices, slots)
    for block in range(BLOCKS):
        here = pl.ds(block, groups, stride=BLOCKS)
        sums = sum_merge(packs, chosen, slots, [block], groups)
        out[here, :] = BACK * (base[here, :] - jnp.log2(sums))


def paired(devices):
    return devices & (devices - 1) == 0


def partner(me, step, devices):
    if paired(devices):
        return jnp.bitwise_xor(me, step)
    return lax.rem(me + devices - step, devices)


def exchange(pack, axis, devices):
    packs = [pack]
    for step in range(1, devices):
        if paired(devices):
            route = [(device, device ^ step) for device in range(devices)]
        else:
            route = [(device, (device + step) % devices) for device in range(devices)]
        packs.append(keep(lax.ppermute(pack, axis, route)))
    return packs


def call(kernel, outs, operands, specs=None, scratch=(), **params):
    return pl.pallas_call(
        kernel,
        out_shape=outs,
        in_specs=specs or [HERE] * len(operands),
        out_specs=jax.tree.map(lambda _: HERE, outs, is_leaf=lambda leaf: not isinstance(leaf, list)),
        scratch_shapes=list(scratch),
        compiler_params=pltpu.CompilerParams(vmem_limit_bytes=16 << 20),
        **params,
    )(*operands)


def bind(kernel, *fixed):
    return lambda *refs: kernel(*fixed, *refs)


def make_body(n_user, n_item):
    def body(user_emb, item_emb, user_count, item_count, tiles, tile_count):
        slots = tiles.shape[2]
        tall = (slots, CLUSTER, CLUSTER)
        groups = user_emb.shape[0] // CLUSTER
        fixed = fixed_slots(groups, n_user, n_item, slots)
        shape = pack_shape(slots, fixed)
        packed = near(shape)
        vectors = near(VECTORS)
        splat = near((ROWS, LANES))
        numbers = near((ROWS, LANES), jnp.int32)
        user_counts = user_count.reshape(-1, LANES)
        item_counts = item_count.reshape(-1, LANES)
        gathered = near((slots, CLUSTER, user_emb.shape[1]), user_emb.dtype)

        small = pltpu.SMEM((2, slots), jnp.int32)
        far_tiles = jnp.transpose(tiles, (0, 1, 3, 2)).reshape(2, slots)
        pack, users, items = call(
            bind(first_kernel, (n_user, n_item)),
            [packed, gathered, gathered],
            (
                away(far_tiles), tile_count, away(user_emb), away(item_emb), away(item_counts),
            ),
            [FAR, SCALARS, FAR, FAR, FAR],
            [
                small,
                near(item_counts.shape, jnp.int32),
                pltpu.SemaphoreType.DMA((2,)),
                pltpu.SemaphoreType.DMA((slots, 2)),
            ],
        )
        first_packs = exchange(pack, "item", n_item)
        table, user_here, item_here, user_ids, item_ids, notes, active = call(
            bind(setup_kernel, (n_user, n_item)),
            [near(tall), vectors, vectors, numbers, numbers, packed, vectors],
            (
                away(far_tiles), tile_count, keep(users), keep(items),
                away(user_counts), away(item_counts),
            ),
            [FAR, SCALARS, HERE, HERE, FAR, FAR],
            [
                small,
                near(user_counts.shape, jnp.int32),
                near(item_counts.shape, jnp.int32),
                pltpu.SemaphoreType.DMA((3,)),
            ],
        )
        pack, terms, tops, user_masks, item_total = call(
            bind(second_kernel, "item", n_item, fixed, groups),
            [packed, near(tall), vectors, near((n_item * slots, ROWS, LANES)), splat],
            (*first_packs, keep(table), user_ids, user_here, notes, active),
            scratch=[near(VECTORS)],
        )
        terms = keep(terms)
        second_packs = exchange(pack, "user", n_user)
        pack, factor, item_masks, user_total = call(
            bind(third_kernel, "user", n_user, fixed, groups),
            [packed, vectors, near((n_user * slots, ROWS, LANES)), splat],
            (*second_packs, terms, tops, item_ids, item_here, item_total),
        )
        item_packs = [second_packs]
        for iteration in range(1, ITERS):
            user_packs = exchange(pack, "item", n_item)
            (pack,) = call(
                bind(user_kernel, n_item),
                [packed],
                (*user_packs, terms, user_masks, user_here, user_total, factor),
                scratch=[near(VECTORS)],
            )
            item_packs.append(exchange(pack, "user", n_user))
            if iteration < ITERS - 1:
                pack, factor = call(
                    bind(item_kernel, n_user),
                    [packed, vectors],
                    (*item_packs[-1], terms, item_masks, item_here, item_total, factor),
                )
        user_values = call(
            bind(user_out_kernel, "item", n_item, slots, fixed),
            jax.ShapeDtypeStruct(user_counts.shape, jnp.float32),
            (*first_packs, *user_packs, user_counts, user_total),
            scratch=[near((n_item, *shape)), near((n_item, *shape))],
        )
        middles = ITERS - 2
        base, named = call(
            bind(item_base_kernel, "user", n_user, slots, fixed, middles),
            [near(item_counts.shape), near((n_user * slots, groups, LANES))],
            (*(pack for packs in item_packs[:-1] for pack in packs), item_counts, item_total, user_total),
            scratch=[near((1 + middles, n_user, *shape))],
        )
        item_values = call(
            bind(item_out_kernel, "user", n_user, slots),
            jax.ShapeDtypeStruct(item_counts.shape, jnp.float32),
            (*item_packs[-1], base, named),
            scratch=[near((n_user, *shape))],
        )
        return user_values.reshape(-1), item_values.reshape(-1)

    return body


def solution(mesh):
    in_specs = (
        P(("region", "user"), None),
        P(("region", "item"), None),
        P(("region", "user")),
        P(("region", "item")),
        P(("region", "user"), "item", None, None),
        P(("region", "user"), "item"),
    )
    out_specs = (P(("region", "user")), P(("region", "item")))
    return jax.shard_map(
        make_body(mesh.shape["user"], mesh.shape["item"]),
        mesh=mesh,
        in_specs=in_specs,
        out_specs=out_specs,
        check_vma=False,
    )
```

```python
import functools
import math

import jax
import jax.numpy as jnp
from jax import lax
from jax.experimental import pallas as pl
from jax.experimental.pallas import tpu as pltpu
from jax.sharding import PartitionSpec as P

CLUSTER = 512
LANES = 128
BLOCKS = CLUSTER // LANES
ROWS = 8
STRIP = 32
ITERS = 3
entropy = 0.25
lowest = -1e30
INTO = math.log2(math.e) / entropy
BACK = entropy * math.log(2.0)

HERE = pl.BlockSpec(memory_space=pltpu.VMEM)
SCALARS = pl.BlockSpec(memory_space=pltpu.SMEM)
FAR = pl.BlockSpec(memory_space=pltpu.HBM)
VECTORS = (ROWS, CLUSTER)
EVERY = range(BLOCKS)


def near(shape, dtype=jnp.float32):
    return pltpu.VMEM(shape, dtype)


def keep(array):
    return pltpu.with_memory_space_constraint(array, pltpu.VMEM)


def away(array):
    return pltpu.with_memory_space_constraint(array, pltpu.HBM)


def fixed_slots(groups, n_user, n_item, slots):
    return min(groups // n_user, groups // n_item, slots)


def pack_shape(slots, fixed):
    rows = slots * BLOCKS + slots - fixed + 1
    return (rows + ROWS - 1) // ROWS * ROWS, LANES


def note(slots, number):
    row = slots * BLOCKS + number
    return slice(row, row + 1)


def part_of(block):
    return slice(block * LANES, (block + 1) * LANES)


def put(pack, slot, values):
    for block in EVERY:
        row = slot * BLOCKS + block
        pack[row : row + 1, :] = values[:, part_of(block)]


def get(pack, slot, blocks):
    rows = (slot * BLOCKS + block for block in blocks)
    return jnp.concatenate([pack[row : row + 1, :] for row in rows], axis=1)


def clear_notes(pack, slots):
    rows = pack.shape[0] - slots * BLOCKS
    pack[slots * BLOCKS :, :] = jnp.zeros((rows, LANES), jnp.float32)


def wide(block):
    return jnp.concatenate([block] * BLOCKS, axis=1)


def total_of(counts):
    total = jnp.sum(jnp.sum(counts.astype(jnp.float32), axis=0, keepdims=True), axis=1, keepdims=True)
    return jnp.broadcast_to(total, (1, LANES))


def write_notes(pack, tiles, fixed, which, counts):
    slots = tiles.shape[1]
    clear_notes(pack, slots)
    for slot in range(fixed, slots):
        number = jnp.full((1, LANES), tiles[which, slot], jnp.int32)
        pack[note(slots, slot - fixed), :] = number.astype(jnp.float32)
    pack[note(slots, slots - fixed), :] = total_of(counts)


def staggered(slots, raise_top, add_mass):
    top = raise_top(0)
    for slot in range(1, slots):
        later = raise_top(slot)
        add_mass(slot - 1, top)
        top = later
    add_mass(slots - 1, top)


def first_kernel(
    devices, far_tiles, filled, user_emb, item_emb, far_count, pack, users, items,
    tiles, item_count, small_sems, sems,
):
    slots = tiles.shape[1]
    groups = user_emb.shape[0] // CLUSTER
    small = [
        pltpu.make_async_copy(source, target, small_sems.at[index])
        for index, (source, target) in enumerate(
            ((far_tiles, tiles), (far_count, item_count))
        )
    ]
    for copy in small:
        copy.start()

    def fetch(slot, groups_here):
        pair = []
        for which, (table, into) in enumerate(((user_emb, users), (item_emb, items))):
            start = pl.multiple_of(groups_here[which] * CLUSTER, CLUSTER)
            copy = pltpu.make_async_copy(
                table.at[pl.ds(start, CLUSTER)], into.at[slot], sems.at[slot, which]
            )
            copy.start()
            pair.append(copy)
        return pair

    n_user, n_item = devices
    fixed = fixed_slots(groups, n_user, n_item, slots)
    row, column = lax.axis_index("user"), lax.axis_index("item")
    copies = [
        fetch(slot, [lax.rem(place * fixed + slot, groups) for place in (column, row)])
        for slot in range(fixed)
    ]
    for copy in small:
        copy.wait()
    for slot in range(fixed, slots):
        copies.append(fetch(slot, [tiles[which, slot] for which in range(2)]))
    write_notes(pack, tiles, fixed, 0, item_count[...])
    early = max(1, 3 * fixed // 4)

    for slot in range(slots):
        if slot in (0, early):
            for pair in copies[:early] if slot == 0 else copies[early:]:
                for copy in pair:
                    copy.wait()
        scores = lax.dot_general(
            items[slot], users[slot], (((1,), (1,)), ((), ())), preferred_element_type=jnp.float32
        ) * INTO
        tops, masses = [], []
        for row in range(0, CLUSTER, STRIP):
            part = scores[row : row + STRIP].reshape(STRIP // 8, 8, CLUSTER)
            tops.append(jnp.max(part, axis=0))
            masses.append(jnp.sum(jnp.exp2(part - tops[-1]), axis=0))
        top = jnp.max(functools.reduce(jnp.maximum, tops), axis=0, keepdims=True)
        mass = sum(mass * jnp.exp2(old - top) for mass, old in zip(masses, tops))
        log_mass = top + jnp.log2(jnp.sum(mass, axis=0, keepdims=True))
        put(pack, slot, jnp.where(filled[0, 0] > slot, log_mass, lowest))


def setup_kernel(
    devices, far_tiles, filled, users, items, far_users, far_items,
    table, user_here, item_here, user_ids, item_ids, notes, active, user_log, item_log,
    tiles, user_count, item_count, sems,
):
    slots = tiles.shape[1]
    copies = [
        pltpu.make_async_copy(source, target, sems.at[index])
        for index, (source, target) in enumerate(
            (
                (far_tiles, tiles),
                (far_users, user_count),
                (far_items, item_count),
            )
        )
    ]
    for copy in copies:
        copy.start()
    for slot in range(slots):
        item_block = items[slot]
        for block in range(BLOCKS):
            rows = slice(block * LANES, (block + 1) * LANES)
            table[slot, rows, :] = lax.dot_general(
                users[slot, rows, :], item_block, (((1,), (1,)), ((), ())),
                preferred_element_type=jnp.float32,
            ) * INTO
    for copy in copies:
        copy.wait()
    place = lax.broadcasted_iota(jnp.int32, (ROWS, LANES), 0)
    on = jnp.where(place < filled[0, 0], 1.0, 0.0)
    active[...] = wide(on)
    for which, (counts, here, ids) in enumerate(
        ((user_count, user_here, user_ids), (item_count, item_here, item_ids))
    ):
        numbers = jnp.full((ROWS, LANES), -1, jnp.int32)
        here[...] = jnp.ones(VECTORS, jnp.float32)
        for slot in range(slots):
            group = tiles[which, slot]
            numbers = jnp.where(place == slot, group, numbers)
            for block in range(BLOCKS):
                here[slot : slot + 1, block * LANES : (block + 1) * LANES] = counts[
                    pl.ds(group * BLOCKS + block, 1), :
                ].astype(jnp.float32)
        ids[...] = numbers
        (user_log, item_log)[which][...] = jnp.log2(here[...])
    fixed = fixed_slots(user_count.shape[0] // BLOCKS, *devices, slots)
    write_notes(notes, tiles, fixed, 1, user_count[...])


def matches(packs, owners, ids, slots, fixed, groups):
    chosen = []
    for pack, owner in zip(packs, owners):
        masks = [ids == (owner * fixed + slot) % groups for slot in range(fixed)]
        for number in range(slots - fixed):
            masks.append(ids == pack[note(slots, number), :].astype(jnp.int32))
        chosen.append(masks)
    return chosen


def across(mask, blocks):
    return jnp.concatenate([mask] * len(blocks), axis=1)


def log_merge(packs, chosen, slots, blocks, rows):
    width = len(blocks) * LANES
    top = jnp.full((rows, width), lowest, jnp.float32)
    for pack, masks in zip(packs, chosen):
        for slot in range(slots):
            part = jnp.where(across(masks[slot], blocks), get(pack, slot, blocks), lowest)
            top = jnp.maximum(top, part)
    mass = jnp.zeros((rows, width), jnp.float32)
    for pack, masks in zip(packs, chosen):
        for slot in range(slots):
            part = jnp.exp2(get(pack, slot, blocks) - top)
            mass += jnp.where(across(masks[slot], blocks), part, 0.0)
    return top + jnp.log2(jnp.where(mass > 0.0, mass, 1.0))


def sum_merge(packs, chosen, slots, blocks, rows):
    total = jnp.zeros((rows, len(blocks) * LANES), jnp.float32)
    for pack, masks in zip(packs, chosen):
        for slot in range(slots):
            total += jnp.where(across(masks[slot], blocks), get(pack, slot, blocks), 0.0)
    return total


def total_in(packs, slots, fixed):
    row = note(slots, slots - fixed)
    total = packs[0][row, :]
    for pack in packs[1:]:
        total = total + pack[row, :]
    return total


def owners_of(axis, devices):
    me = lax.axis_index(axis)
    return [partner(me, step, devices) for step in range(devices)]


def store_masks(masks, chosen):
    for index, mask in enumerate(mask for group in chosen for mask in group):
        masks[index] = jnp.where(mask, 1.0, 0.0)


def load_masks(masks, devices, slots):
    return [
        [masks[device * slots + slot] > 0.0 for slot in range(slots)] for device in range(devices)
    ]


def down_rows(vector, slot, block):
    row = vector[slot : slot + 1, block * LANES : (block + 1) * LANES]
    return jnp.broadcast_to(row, (LANES, LANES)).T


def second_kernel(axis, devices, fixed, groups, *refs):
    packs = refs[:devices]
    table, ids, log_counts, notes, active, pack, terms, tops, masks, totals, potential = refs[devices:]
    slots = table.shape[0]
    chosen = matches(packs, owners_of(axis, devices), ids[...], slots, fixed, groups)
    store_masks(masks, chosen)
    totals[...] = jnp.broadcast_to(total_in(packs, slots, fixed), totals.shape)
    potential[...] = log_counts[...] - log_merge(packs, chosen, slots, EVERY, ROWS)
    pack[...] = notes[...]
    tops[...] = jnp.full(VECTORS, lowest, jnp.float32)

    def raise_top(slot):
        top = jnp.full((8, CLUSTER), lowest, jnp.float32)
        for block in range(BLOCKS):
            rows = slice(block * LANES, (block + 1) * LANES)
            part = table[slot, rows, :] + wide(down_rows(potential, slot, block))
            terms[slot, rows, :] = part
            top = jnp.maximum(top, jnp.max(part.reshape(LANES // 8, 8, CLUSTER), axis=0))
        return jnp.max(top, axis=0, keepdims=True)

    def add_mass(slot, top):
        mass = jnp.zeros((8, CLUSTER), jnp.float32)
        for block in range(BLOCKS):
            rows = slice(block * LANES, (block + 1) * LANES)
            part = jnp.exp2(terms[slot, rows, :] - top)
            terms[slot, rows, :] = part
            mass += jnp.sum(part.reshape(LANES // 8, 8, CLUSTER), axis=0)
        log_mass = top + jnp.log2(jnp.sum(mass, axis=0, keepdims=True))
        on = active[slot : slot + 1, :] > 0.0
        put(pack, slot, jnp.where(on, log_mass, lowest))
        tops[slot : slot + 1, :] = jnp.where(on, top, lowest)

    staggered(slots, raise_top, add_mass)


def row_sums(terms, factor, pack):
    slots = terms.shape[0]
    clear_notes(pack, slots)
    for slot in range(slots):
        for block in range(BLOCKS):
            rows = slice(block * LANES, (block + 1) * LANES)
            part = terms[slot, rows, 0:LANES] * factor[slot : slot + 1, 0:LANES]
            for other in range(1, BLOCKS):
                lanes = slice(other * LANES, (other + 1) * LANES)
                part += terms[slot, rows, lanes] * factor[slot : slot + 1, lanes]
            row = slot * BLOCKS + block
            pack[row : row + 1, :] = jnp.sum(part.T, axis=0, keepdims=True)


def column_sums(terms, factor, scale, pack):
    slots = terms.shape[0]
    clear_notes(pack, slots)
    for slot in range(slots):
        mass = jnp.zeros((8, CLUSTER), jnp.float32)
        for block in range(BLOCKS):
            rows = slice(block * LANES, (block + 1) * LANES)
            part = terms[slot, rows, :] * wide(down_rows(factor, slot, block))
            mass += jnp.sum(part.reshape(LANES // 8, 8, CLUSTER), axis=0)
        put(pack, slot, jnp.sum(mass, axis=0, keepdims=True) * scale[slot : slot + 1, :])


def third_kernel(axis, devices, fixed, groups, *refs):
    packs = refs[:devices]
    terms, tops, ids, log_counts, item_total, pack, factor, masks, totals = refs[devices:]
    slots = terms.shape[0]
    chosen = matches(packs, owners_of(axis, devices), ids[...], slots, fixed, groups)
    store_masks(masks, chosen)
    totals[...] = jnp.broadcast_to(total_in(packs, slots, fixed), totals.shape)
    log_share = log_counts[...] - wide(jnp.log2(item_total[...]))
    merged = log_merge(packs, chosen, slots, EVERY, ROWS)
    factor[...] = jnp.exp2(tops[...] + (log_share - merged))
    row_sums(terms, factor, pack)


def user_kernel(devices, *refs):
    packs = refs[:devices]
    terms, masks, counts, totals, scale, pack, factor = refs[devices:]
    slots = terms.shape[0]
    sums = sum_merge(packs, load_masks(masks, devices, slots), slots, EVERY, ROWS)
    factor[...] = counts[...] / (wide(totals[...]) * jnp.where(sums > 0.0, sums, 1.0))
    column_sums(terms, factor, scale, pack)


def item_kernel(devices, *refs):
    packs = refs[:devices]
    terms, masks, counts, totals, old, pack, factor = refs[devices:]
    slots = terms.shape[0]
    sums = sum_merge(packs, load_masks(masks, devices, slots), slots, EVERY, ROWS)
    share = counts[...] / (wide(totals[...]) * jnp.where(sums > 0.0, sums, 1.0))
    factor[...] = old[...] * share
    row_sums(terms, factor, pack)


def in_order(axis, devices, packs, ordered):
    me = lax.axis_index(axis)
    for step in range(devices):
        ordered[partner(me, step, devices)] = packs[step][...]
    return [ordered.at[device] for device in range(devices)]


def cluster_matches(packs, slots, fixed, groups):
    numbers = lax.broadcasted_iota(jnp.int32, (groups, LANES), 0)
    return matches(packs, range(len(packs)), numbers, slots, fixed, groups)


def user_out_kernel(axis, devices, slots, fixed, *refs):
    counts, totals, out, first_packs, last_packs = refs[2 * devices :]
    first = in_order(axis, devices, refs[:devices], first_packs)
    last = in_order(axis, devices, refs[devices : 2 * devices], last_packs)
    groups = counts.shape[0] // BLOCKS
    chosen = cluster_matches(first, slots, fixed, groups)
    for block in range(BLOCKS):
        here = pl.ds(block, groups, stride=BLOCKS)
        share = jnp.log2(counts[here, :].astype(jnp.float32) / totals[0:1, :])
        merged = log_merge(first, chosen, slots, [block], groups)
        sums = sum_merge(last, chosen, slots, [block], groups)
        out[here, :] = BACK * (2.0 * share - merged - jnp.log2(sums))


def item_base_kernel(axis, devices, slots, fixed, middles, *refs):
    given = (1 + middles) * devices
    counts, item_total, user_total, out, numbers, all_packs = refs[given:]
    packs = [
        in_order(axis, devices, refs[step * devices : (step + 1) * devices], all_packs.at[step])
        for step in range(1 + middles)
    ]
    groups = counts.shape[0] // BLOCKS
    chosen = cluster_matches(packs[0], slots, fixed, groups)
    for index, mask in enumerate(mask for group in chosen for mask in group):
        numbers[index] = jnp.where(mask, 1.0, 0.0)
    for block in range(BLOCKS):
        here = pl.ds(block, groups, stride=BLOCKS)
        share = jnp.log2(counts[here, :].astype(jnp.float32) / item_total[0:1, :])
        base = (2 + middles) * share + jnp.log2(user_total[0:1, :])
        base = base - log_merge(packs[0], chosen, slots, [block], groups)
        for step in range(middles):
            base = base - jnp.log2(sum_merge(packs[1 + step], chosen, slots, [block], groups))
        out[here, :] = base


def item_out_kernel(axis, devices, slots, *refs):
    base, numbers, out, packs_here = refs[devices:]
    packs = in_order(axis, devices, refs[:devices], packs_here)
    groups = base.shape[0] // BLOCKS
    chosen = load_masks(numbers, devices, slots)
    for block in range(BLOCKS):
        here = pl.ds(block, groups, stride=BLOCKS)
        sums = sum_merge(packs, chosen, slots, [block], groups)
        out[here, :] = BACK * (base[here, :] - jnp.log2(sums))


def paired(devices):
    return devices & (devices - 1) == 0


def partner(me, step, devices):
    if paired(devices):
        return jnp.bitwise_xor(me, step)
    return lax.rem(me + devices - step, devices)


def exchange(pack, axis, devices):
    packs = [pack]
    for step in range(1, devices):
        if paired(devices):
            route = [(device, device ^ step) for device in range(devices)]
        else:
            route = [(device, (device + step) % devices) for device in range(devices)]
        packs.append(keep(lax.ppermute(pack, axis, route)))
    return packs


def call(kernel, outs, operands, specs=None, scratch=(), **params):
    return pl.pallas_call(
        kernel,
        out_shape=outs,
        in_specs=specs or [HERE] * len(operands),
        out_specs=jax.tree.map(lambda _: HERE, outs, is_leaf=lambda leaf: not isinstance(leaf, list)),
        scratch_shapes=list(scratch),
        compiler_params=pltpu.CompilerParams(vmem_limit_bytes=16 << 20),
        **params,
    )(*operands)


def bind(kernel, *fixed):
    return lambda *refs: kernel(*fixed, *refs)


def make_body(n_user, n_item):
    def body(user_emb, item_emb, user_count, item_count, tiles, tile_count):
        slots = tiles.shape[2]
        tall = (slots, CLUSTER, CLUSTER)
        groups = user_emb.shape[0] // CLUSTER
        fixed = fixed_slots(groups, n_user, n_item, slots)
        shape = pack_shape(slots, fixed)
        packed = near(shape)
        vectors = near(VECTORS)
        splat = near((ROWS, LANES))
        numbers = near((ROWS, LANES), jnp.int32)
        user_counts = user_count.reshape(-1, LANES)
        item_counts = item_count.reshape(-1, LANES)
        gathered = near((slots, CLUSTER, user_emb.shape[1]), user_emb.dtype)

        small = pltpu.SMEM((2, slots), jnp.int32)
        far_tiles = jnp.transpose(tiles, (0, 1, 3, 2)).reshape(2, slots)
        pack, users, items = call(
            bind(first_kernel, (n_user, n_item)),
            [packed, gathered, gathered],
            (
                away(far_tiles), tile_count, away(user_emb), away(item_emb), away(item_counts),
            ),
            [FAR, SCALARS, FAR, FAR, FAR],
            [
                small,
                near(item_counts.shape, jnp.int32),
                pltpu.SemaphoreType.DMA((2,)),
                pltpu.SemaphoreType.DMA((slots, 2)),
            ],
        )
        first_packs = exchange(pack, "item", n_item)
        table, user_here, item_here, user_ids, item_ids, notes, active, user_log, item_log = call(
            bind(setup_kernel, (n_user, n_item)),
            [near(tall), vectors, vectors, numbers, numbers, packed, vectors, vectors, vectors],
            (
                away(far_tiles), tile_count, keep(users), keep(items),
                away(user_counts), away(item_counts),
            ),
            [FAR, SCALARS, HERE, HERE, FAR, FAR],
            [
                small,
                near(user_counts.shape, jnp.int32),
                near(item_counts.shape, jnp.int32),
                pltpu.SemaphoreType.DMA((3,)),
            ],
        )
        pack, terms, tops, user_masks, item_total = call(
            bind(second_kernel, "item", n_item, fixed, groups),
            [packed, near(tall), vectors, near((n_item * slots, ROWS, LANES)), splat],
            (*first_packs, keep(table), user_ids, user_log, notes, active),
            scratch=[near(VECTORS)],
        )
        terms = keep(terms)
        second_packs = exchange(pack, "user", n_user)
        pack, factor, item_masks, user_total = call(
            bind(third_kernel, "user", n_user, fixed, groups),
            [packed, vectors, near((n_user * slots, ROWS, LANES)), splat],
            (*second_packs, terms, tops, item_ids, item_log, item_total),
        )
        item_packs = [second_packs]
        for iteration in range(1, ITERS):
            user_packs = exchange(pack, "item", n_item)
            (pack,) = call(
                bind(user_kernel, n_item),
                [packed],
                (*user_packs, terms, user_masks, user_here, user_total, factor),
                scratch=[near(VECTORS)],
            )
            item_packs.append(exchange(pack, "user", n_user))
            if iteration < ITERS - 1:
                pack, factor = call(
                    bind(item_kernel, n_user),
                    [packed, vectors],
                    (*item_packs[-1], terms, item_masks, item_here, item_total, factor),
                )
        user_values = call(
            bind(user_out_kernel, "item", n_item, slots, fixed),
            jax.ShapeDtypeStruct(user_counts.shape, jnp.float32),
            (*first_packs, *user_packs, user_counts, user_total),
            scratch=[near((n_item, *shape)), near((n_item, *shape))],
        )
        middles = ITERS - 2
        base, named = call(
            bind(item_base_kernel, "user", n_user, slots, fixed, middles),
            [near(item_counts.shape), near((n_user * slots, groups, LANES))],
            (*(pack for packs in item_packs[:-1] for pack in packs), item_counts, item_total, user_total),
            scratch=[near((1 + middles, n_user, *shape))],
        )
        item_values = call(
            bind(item_out_kernel, "user", n_user, slots),
            jax.ShapeDtypeStruct(item_counts.shape, jnp.float32),
            (*item_packs[-1], base, named),
            scratch=[near((n_user, *shape))],
        )
        return user_values.reshape(-1), item_values.reshape(-1)

    return body


def solution(mesh):
    in_specs = (
        P(("region", "user"), None),
        P(("region", "item"), None),
        P(("region", "user")),
        P(("region", "item")),
        P(("region", "user"), "item", None, None),
        P(("region", "user"), "item"),
    )
    out_specs = (P(("region", "user")), P(("region", "item")))
    return jax.shard_map(
        make_body(mesh.shape["user"], mesh.shape["item"]),
        mesh=mesh,
        in_specs=in_specs,
        out_specs=out_specs,
        check_vma=False,
    )
```

```python
import functools
import math

import jax
import jax.numpy as jnp
from jax import lax
from jax.experimental import pallas as pl
from jax.experimental.pallas import tpu as pltpu
from jax.sharding import PartitionSpec as P

CLUSTER = 512
LANES = 128
BLOCKS = CLUSTER // LANES
ROWS = 8
STRIP = 32
ITERS = 3
entropy = 0.25
lowest = -1e30
INTO = math.log2(math.e) / entropy
BACK = entropy * math.log(2.0)

HERE = pl.BlockSpec(memory_space=pltpu.VMEM)
SCALARS = pl.BlockSpec(memory_space=pltpu.SMEM)
FAR = pl.BlockSpec(memory_space=pltpu.HBM)
VECTORS = (ROWS, CLUSTER)
EVERY = range(BLOCKS)


def near(shape, dtype=jnp.float32):
    return pltpu.VMEM(shape, dtype)


def keep(array):
    return pltpu.with_memory_space_constraint(array, pltpu.VMEM)


def away(array):
    return pltpu.with_memory_space_constraint(array, pltpu.HBM)


def fixed_slots(groups, n_user, n_item, slots):
    return min(groups // n_user, groups // n_item, slots)


def pack_shape(slots, fixed):
    rows = slots * BLOCKS + slots - fixed + 1
    return (rows + ROWS - 1) // ROWS * ROWS, LANES


def note(slots, number):
    row = slots * BLOCKS + number
    return slice(row, row + 1)


def part_of(block):
    return slice(block * LANES, (block + 1) * LANES)


def put(pack, slot, values):
    for block in EVERY:
        row = slot * BLOCKS + block
        pack[row : row + 1, :] = values[:, part_of(block)]


def get(pack, slot, blocks):
    rows = (slot * BLOCKS + block for block in blocks)
    return jnp.concatenate([pack[row : row + 1, :] for row in rows], axis=1)


def clear_notes(pack, slots):
    rows = pack.shape[0] - slots * BLOCKS
    pack[slots * BLOCKS :, :] = jnp.zeros((rows, LANES), jnp.float32)


def wide(block):
    return jnp.concatenate([block] * BLOCKS, axis=1)


def total_of(counts):
    total = jnp.sum(jnp.sum(counts.astype(jnp.float32), axis=0, keepdims=True), axis=1, keepdims=True)
    return jnp.broadcast_to(total, (1, LANES))


def write_notes(pack, tiles, fixed, which, counts):
    slots = tiles.shape[1]
    clear_notes(pack, slots)
    for slot in range(fixed, slots):
        number = jnp.full((1, LANES), tiles[which, slot], jnp.int32)
        pack[note(slots, slot - fixed), :] = number.astype(jnp.float32)
    pack[note(slots, slots - fixed), :] = total_of(counts)


def staggered(slots, raise_top, add_mass):
    top = raise_top(0)
    for slot in range(1, slots):
        later = raise_top(slot)
        add_mass(slot - 1, top)
        top = later
    add_mass(slots - 1, top)


def first_kernel(
    devices, far_tiles, filled, user_emb, item_emb, far_count, pack, users, items,
    tiles, item_count, small_sems, sems,
):
    slots = tiles.shape[1]
    groups = user_emb.shape[0] // CLUSTER
    small = [
        pltpu.make_async_copy(source, target, small_sems.at[index])
        for index, (source, target) in enumerate(
            ((far_tiles, tiles), (far_count, item_count))
        )
    ]
    for copy in small:
        copy.start()

    def fetch(slot, groups_here):
        pair = []
        for which, (table, into) in enumerate(((user_emb, users), (item_emb, items))):
            start = pl.multiple_of(groups_here[which] * CLUSTER, CLUSTER)
            copy = pltpu.make_async_copy(
                table.at[pl.ds(start, CLUSTER)], into.at[slot], sems.at[slot, which]
            )
            copy.start()
            pair.append(copy)
        return pair

    n_user, n_item = devices
    fixed = fixed_slots(groups, n_user, n_item, slots)
    row, column = lax.axis_index("user"), lax.axis_index("item")
    copies = [
        fetch(slot, [lax.rem(place * fixed + slot, groups) for place in (column, row)])
        for slot in range(fixed)
    ]
    for copy in small:
        copy.wait()
    for slot in range(fixed, slots):
        copies.append(fetch(slot, [tiles[which, slot] for which in range(2)]))
    write_notes(pack, tiles, fixed, 0, item_count[...])
    early = max(1, 3 * fixed // 4)

    for slot in range(slots):
        if slot in (0, early):
            for pair in copies[:early] if slot == 0 else copies[early:]:
                for copy in pair:
                    copy.wait()
        scores = lax.dot_general(
            items[slot], users[slot], (((1,), (1,)), ((), ())), preferred_element_type=jnp.float32
        ) * INTO
        tops, masses = [], []
        for row in range(0, CLUSTER, STRIP):
            part = scores[row : row + STRIP].reshape(STRIP // 8, 8, CLUSTER)
            tops.append(jnp.max(part, axis=0))
            masses.append(jnp.sum(jnp.exp2(part - tops[-1]), axis=0))
        top = jnp.max(functools.reduce(jnp.maximum, tops), axis=0, keepdims=True)
        mass = sum(mass * jnp.exp2(old - top) for mass, old in zip(masses, tops))
        log_mass = top + jnp.log2(jnp.sum(mass, axis=0, keepdims=True))
        put(pack, slot, jnp.where(filled[0, 0] > slot, log_mass, lowest))


def setup_kernel(
    devices, far_tiles, filled, users, items, far_users, far_items,
    table, user_here, item_here, user_ids, item_ids, notes, active, user_log, item_log,
    tiles, user_count, item_count, sems,
):
    slots = tiles.shape[1]
    copies = [
        pltpu.make_async_copy(source, target, sems.at[index])
        for index, (source, target) in enumerate(
            (
                (far_tiles, tiles),
                (far_users, user_count),
                (far_items, item_count),
            )
        )
    ]
    for copy in copies:
        copy.start()
    for slot in range(slots):
        item_block = items[slot]
        for block in range(BLOCKS):
            rows = slice(block * LANES, (block + 1) * LANES)
            table[slot, rows, :] = lax.dot_general(
                users[slot, rows, :], item_block, (((1,), (1,)), ((), ())),
                preferred_element_type=jnp.float32,
            ) * INTO
    for copy in copies:
        copy.wait()
    place = lax.broadcasted_iota(jnp.int32, (ROWS, LANES), 0)
    on = jnp.where(place < filled[0, 0], 1.0, 0.0)
    active[...] = wide(on)
    for which, (counts, here, ids) in enumerate(
        ((user_count, user_here, user_ids), (item_count, item_here, item_ids))
    ):
        numbers = jnp.full((ROWS, LANES), -1, jnp.int32)
        here[...] = jnp.ones(VECTORS, jnp.float32)
        for slot in range(slots):
            group = tiles[which, slot]
            numbers = jnp.where(place == slot, group, numbers)
            for block in range(BLOCKS):
                here[slot : slot + 1, block * LANES : (block + 1) * LANES] = counts[
                    pl.ds(group * BLOCKS + block, 1), :
                ].astype(jnp.float32)
        ids[...] = numbers
        (user_log, item_log)[which][...] = jnp.log2(here[...])
    fixed = fixed_slots(user_count.shape[0] // BLOCKS, *devices, slots)
    write_notes(notes, tiles, fixed, 1, user_count[...])


def matches(packs, owners, ids, slots, fixed, groups):
    chosen = []
    for pack, owner in zip(packs, owners):
        masks = [ids == (owner * fixed + slot) % groups for slot in range(fixed)]
        for number in range(slots - fixed):
            masks.append(ids == pack[note(slots, number), :].astype(jnp.int32))
        chosen.append(masks)
    return chosen


def across(mask, blocks):
    return jnp.concatenate([mask] * len(blocks), axis=1)


def log_merge(packs, chosen, slots, blocks, rows):
    width = len(blocks) * LANES
    top = jnp.full((rows, width), lowest, jnp.float32)
    for pack, masks in zip(packs, chosen):
        for slot in range(slots):
            part = jnp.where(across(masks[slot], blocks), get(pack, slot, blocks), lowest)
            top = jnp.maximum(top, part)
    mass = jnp.zeros((rows, width), jnp.float32)
    for pack, masks in zip(packs, chosen):
        for slot in range(slots):
            part = jnp.exp2(get(pack, slot, blocks) - top)
            mass += jnp.where(across(masks[slot], blocks), part, 0.0)
    return top + jnp.log2(jnp.where(mass > 0.0, mass, 1.0))


def sum_merge(packs, chosen, slots, blocks, rows):
    total = jnp.zeros((rows, len(blocks) * LANES), jnp.float32)
    for pack, masks in zip(packs, chosen):
        for slot in range(slots):
            total += jnp.where(across(masks[slot], blocks), get(pack, slot, blocks), 0.0)
    return total


def total_in(packs, slots, fixed):
    row = note(slots, slots - fixed)
    total = packs[0][row, :]
    for pack in packs[1:]:
        total = total + pack[row, :]
    return total


def owners_of(axis, devices):
    me = lax.axis_index(axis)
    return [partner(me, step, devices) for step in range(devices)]


def store_masks(masks, chosen):
    for index, mask in enumerate(mask for group in chosen for mask in group):
        masks[index] = jnp.where(mask, 1.0, 0.0)


def load_masks(masks, devices, slots):
    return [
        [masks[device * slots + slot] > 0.0 for slot in range(slots)] for device in range(devices)
    ]


def down_rows(vector, slot, block):
    row = vector[slot : slot + 1, block * LANES : (block + 1) * LANES]
    return jnp.broadcast_to(row, (LANES, LANES)).T


def second_kernel(axis, devices, fixed, groups, *refs):
    packs = refs[:devices]
    table, ids, log_counts, notes, active, pack, terms, tops, masks, totals, potential = refs[devices:]
    slots = table.shape[0]
    chosen = matches(packs, owners_of(axis, devices), ids[...], slots, fixed, groups)
    store_masks(masks, chosen)
    totals[...] = jnp.broadcast_to(total_in(packs, slots, fixed), totals.shape)
    potential[...] = log_counts[...] - log_merge(packs, chosen, slots, EVERY, ROWS)
    pack[...] = notes[...]
    tops[...] = jnp.full(VECTORS, lowest, jnp.float32)

    def raise_top(slot):
        top = jnp.full((8, CLUSTER), lowest, jnp.float32)
        for block in range(BLOCKS):
            rows = slice(block * LANES, (block + 1) * LANES)
            part = table[slot, rows, :] + wide(down_rows(potential, slot, block))
            terms[slot, rows, :] = part
            top = jnp.maximum(top, jnp.max(part.reshape(LANES // 8, 8, CLUSTER), axis=0))
        return jnp.max(top, axis=0, keepdims=True)

    def add_mass(slot, top):
        mass = jnp.zeros((8, CLUSTER), jnp.float32)
        for block in range(BLOCKS):
            rows = slice(block * LANES, (block + 1) * LANES)
            part = jnp.exp2(terms[slot, rows, :] - top)
            terms[slot, rows, :] = part
            mass += jnp.sum(part.reshape(LANES // 8, 8, CLUSTER), axis=0)
        log_mass = top + jnp.log2(jnp.sum(mass, axis=0, keepdims=True))
        on = active[slot : slot + 1, :] > 0.0
        put(pack, slot, jnp.where(on, log_mass, lowest))
        tops[slot : slot + 1, :] = jnp.where(on, top, lowest)

    staggered(slots, raise_top, add_mass)


def row_sums(terms, factor, pack):
    slots = terms.shape[0]
    clear_notes(pack, slots)
    for slot in range(slots):
        for block in range(BLOCKS):
            rows = slice(block * LANES, (block + 1) * LANES)
            part = terms[slot, rows, 0:LANES] * factor[slot : slot + 1, 0:LANES]
            for other in range(1, BLOCKS):
                lanes = slice(other * LANES, (other + 1) * LANES)
                part += terms[slot, rows, lanes] * factor[slot : slot + 1, lanes]
            row = slot * BLOCKS + block
            pack[row : row + 1, :] = jnp.sum(part.T, axis=0, keepdims=True)


def column_sums(terms, factor, scale, pack):
    slots = terms.shape[0]
    clear_notes(pack, slots)
    for slot in range(slots):
        mass = jnp.zeros((8, CLUSTER), jnp.float32)
        for block in range(BLOCKS):
            rows = slice(block * LANES, (block + 1) * LANES)
            part = terms[slot, rows, :] * wide(down_rows(factor, slot, block))
            mass += jnp.sum(part.reshape(LANES // 8, 8, CLUSTER), axis=0)
        put(pack, slot, jnp.sum(mass, axis=0, keepdims=True) * scale[slot : slot + 1, :])


def third_kernel(axis, devices, fixed, groups, *refs):
    packs = refs[:devices]
    terms, tops, ids, log_counts, item_total, pack, factor, masks, totals = refs[devices:]
    slots = terms.shape[0]
    chosen = matches(packs, owners_of(axis, devices), ids[...], slots, fixed, groups)
    store_masks(masks, chosen)
    totals[...] = jnp.broadcast_to(total_in(packs, slots, fixed), totals.shape)
    log_share = log_counts[...] - wide(jnp.log2(item_total[...]))
    merged = log_merge(packs, chosen, slots, EVERY, ROWS)
    factor[...] = jnp.exp2(tops[...] + (log_share - merged))
    row_sums(terms, factor, pack)


def user_kernel(devices, *refs):
    packs = refs[:devices]
    terms, masks, counts, totals, scale, pack, factor = refs[devices:]
    slots = terms.shape[0]
    sums = sum_merge(packs, load_masks(masks, devices, slots), slots, EVERY, ROWS)
    factor[...] = counts[...] / (wide(totals[...]) * jnp.where(sums > 0.0, sums, 1.0))
    column_sums(terms, factor, scale, pack)


def item_kernel(devices, *refs):
    packs = refs[:devices]
    terms, masks, counts, totals, old, pack, factor = refs[devices:]
    slots = terms.shape[0]
    sums = sum_merge(packs, load_masks(masks, devices, slots), slots, EVERY, ROWS)
    share = counts[...] / (wide(totals[...]) * jnp.where(sums > 0.0, sums, 1.0))
    factor[...] = old[...] * share
    row_sums(terms, factor, pack)


def in_order(axis, devices, packs, ordered):
    me = lax.axis_index(axis)
    for step in range(devices):
        ordered[partner(me, step, devices)] = packs[step][...]
    return [ordered.at[device] for device in range(devices)]


def cluster_matches(packs, slots, fixed, groups):
    numbers = lax.broadcasted_iota(jnp.int32, (groups, LANES), 0)
    return matches(packs, range(len(packs)), numbers, slots, fixed, groups)


def user_out_kernel(axis, devices, slots, fixed, *refs):
    counts, totals, out, first_packs, last_packs = refs[2 * devices :]
    first = in_order(axis, devices, refs[:devices], first_packs)
    last = in_order(axis, devices, refs[devices : 2 * devices], last_packs)
    groups = counts.shape[0] // BLOCKS
    chosen = cluster_matches(first, slots, fixed, groups)
    for block in range(BLOCKS):
        here = pl.ds(block, groups, stride=BLOCKS)
        share = jnp.log2(counts[here, :].astype(jnp.float32) / totals[0:1, :])
        merged = log_merge(first, chosen, slots, [block], groups)
        sums = sum_merge(last, chosen, slots, [block], groups)
        out[here, :] = BACK * (2.0 * share - merged - jnp.log2(sums))


def item_base_kernel(axis, devices, slots, fixed, middles, *refs):
    given = (1 + middles) * devices
    counts, item_total, user_total, out, numbers, all_packs = refs[given:]
    packs = [
        in_order(axis, devices, refs[step * devices : (step + 1) * devices], all_packs.at[step])
        for step in range(1 + middles)
    ]
    groups = counts.shape[0] // BLOCKS
    chosen = cluster_matches(packs[0], slots, fixed, groups)
    for index, mask in enumerate(mask for group in chosen for mask in group):
        numbers[index] = jnp.where(mask, 1.0, 0.0)
    for block in range(BLOCKS):
        here = pl.ds(block, groups, stride=BLOCKS)
        share = jnp.log2(counts[here, :].astype(jnp.float32) / item_total[0:1, :])
        base = (2 + middles) * share + jnp.log2(user_total[0:1, :])
        base = base - log_merge(packs[0], chosen, slots, [block], groups)
        for step in range(middles):
            base = base - jnp.log2(sum_merge(packs[1 + step], chosen, slots, [block], groups))
        out[here, :] = base


def item_out_kernel(axis, devices, slots, *refs):
    base, numbers, out = refs[devices:]
    given = [pack[...] for pack in refs[:devices]]
    owners = owners_of(axis, devices)
    packs = []
    for device in range(devices):
        chosen = given[0]
        for step in range(1, devices):
            chosen = jnp.where(owners[step] == device, given[step], chosen)
        packs.append(chosen)
    groups = base.shape[0] // BLOCKS
    chosen = load_masks(numbers, devices, slots)
    for block in range(BLOCKS):
        here = pl.ds(block, groups, stride=BLOCKS)
        sums = sum_merge(packs, chosen, slots, [block], groups)
        out[here, :] = BACK * (base[here, :] - jnp.log2(sums))


def paired(devices):
    return devices & (devices - 1) == 0


def partner(me, step, devices):
    if paired(devices):
        return jnp.bitwise_xor(me, step)
    return lax.rem(me + devices - step, devices)


def exchange(pack, axis, devices):
    packs = [pack]
    for step in range(1, devices):
        if paired(devices):
            route = [(device, device ^ step) for device in range(devices)]
        else:
            route = [(device, (device + step) % devices) for device in range(devices)]
        packs.append(keep(lax.ppermute(pack, axis, route)))
    return packs


def call(kernel, outs, operands, specs=None, scratch=(), **params):
    return pl.pallas_call(
        kernel,
        out_shape=outs,
        in_specs=specs or [HERE] * len(operands),
        out_specs=jax.tree.map(lambda _: HERE, outs, is_leaf=lambda leaf: not isinstance(leaf, list)),
        scratch_shapes=list(scratch),
        compiler_params=pltpu.CompilerParams(vmem_limit_bytes=16 << 20),
        **params,
    )(*operands)


def bind(kernel, *fixed):
    return lambda *refs: kernel(*fixed, *refs)


def make_body(n_user, n_item):
    def body(user_emb, item_emb, user_count, item_count, tiles, tile_count):
        slots = tiles.shape[2]
        tall = (slots, CLUSTER, CLUSTER)
        groups = user_emb.shape[0] // CLUSTER
        fixed = fixed_slots(groups, n_user, n_item, slots)
        shape = pack_shape(slots, fixed)
        packed = near(shape)
        vectors = near(VECTORS)
        splat = near((ROWS, LANES))
        numbers = near((ROWS, LANES), jnp.int32)
        user_counts = user_count.reshape(-1, LANES)
        item_counts = item_count.reshape(-1, LANES)
        gathered = near((slots, CLUSTER, user_emb.shape[1]), user_emb.dtype)

        small = pltpu.SMEM((2, slots), jnp.int32)
        far_tiles = jnp.transpose(tiles, (0, 1, 3, 2)).reshape(2, slots)
        pack, users, items = call(
            bind(first_kernel, (n_user, n_item)),
            [packed, gathered, gathered],
            (
                away(far_tiles), tile_count, away(user_emb), away(item_emb), away(item_counts),
            ),
            [FAR, SCALARS, FAR, FAR, FAR],
            [
                small,
                near(item_counts.shape, jnp.int32),
                pltpu.SemaphoreType.DMA((2,)),
                pltpu.SemaphoreType.DMA((slots, 2)),
            ],
        )
        first_packs = exchange(pack, "item", n_item)
        table, user_here, item_here, user_ids, item_ids, notes, active, user_log, item_log = call(
            bind(setup_kernel, (n_user, n_item)),
            [near(tall), vectors, vectors, numbers, numbers, packed, vectors, vectors, vectors],
            (
                away(far_tiles), tile_count, keep(users), keep(items),
                away(user_counts), away(item_counts),
            ),
            [FAR, SCALARS, HERE, HERE, FAR, FAR],
            [
                small,
                near(user_counts.shape, jnp.int32),
                near(item_counts.shape, jnp.int32),
                pltpu.SemaphoreType.DMA((3,)),
            ],
        )
        pack, terms, tops, user_masks, item_total = call(
            bind(second_kernel, "item", n_item, fixed, groups),
            [packed, near(tall), vectors, near((n_item * slots, ROWS, LANES)), splat],
            (*first_packs, keep(table), user_ids, user_log, notes, active),
            scratch=[near(VECTORS)],
        )
        terms = keep(terms)
        second_packs = exchange(pack, "user", n_user)
        pack, factor, item_masks, user_total = call(
            bind(third_kernel, "user", n_user, fixed, groups),
            [packed, vectors, near((n_user * slots, ROWS, LANES)), splat],
            (*second_packs, terms, tops, item_ids, item_log, item_total),
        )
        item_packs = [second_packs]
        for iteration in range(1, ITERS):
            user_packs = exchange(pack, "item", n_item)
            (pack,) = call(
                bind(user_kernel, n_item),
                [packed],
                (*user_packs, terms, user_masks, user_here, user_total, factor),
                scratch=[near(VECTORS)],
            )
            item_packs.append(exchange(pack, "user", n_user))
            if iteration < ITERS - 1:
                pack, factor = call(
                    bind(item_kernel, n_user),
                    [packed, vectors],
                    (*item_packs[-1], terms, item_masks, item_here, item_total, factor),
                )
        user_values = call(
            bind(user_out_kernel, "item", n_item, slots, fixed),
            jax.ShapeDtypeStruct(user_counts.shape, jnp.float32),
            (*first_packs, *user_packs, user_counts, user_total),
            scratch=[near((n_item, *shape)), near((n_item, *shape))],
        )
        middles = ITERS - 2
        base, named = call(
            bind(item_base_kernel, "user", n_user, slots, fixed, middles),
            [near(item_counts.shape), near((n_user * slots, groups, LANES))],
            (*(pack for packs in item_packs[:-1] for pack in packs), item_counts, item_total, user_total),
            scratch=[near((1 + middles, n_user, *shape))],
        )
        item_values = call(
            bind(item_out_kernel, "user", n_user, slots),
            jax.ShapeDtypeStruct(item_counts.shape, jnp.float32),
            (*item_packs[-1], base, named),
        )
        return user_values.reshape(-1), item_values.reshape(-1)

    return body


def solution(mesh):
    in_specs = (
        P(("region", "user"), None),
        P(("region", "item"), None),
        P(("region", "user")),
        P(("region", "item")),
        P(("region", "user"), "item", None, None),
        P(("region", "user"), "item"),
    )
    out_specs = (P(("region", "user")), P(("region", "item")))
    return jax.shard_map(
        make_body(mesh.shape["user"], mesh.shape["item"]),
        mesh=mesh,
        in_specs=in_specs,
        out_specs=out_specs,
        check_vma=False,
    )
```
